32 devices in a mesh: dp: 4 (over y, x), mp: 8 (over z, core).
Axes of the slice: x: 2, y: 2, z: 4, core: 2. Of those that a mesh axis runs over, the one named last changes fastest.
Arguments:
- out_grads: bfloat16 [512, 28672], P('dp', 'mp'), may hold values from -6 to 6
- inputs: bfloat16 [512, 8192], P('mp', 'dp'), may hold values from -6 to 6
- out_basis: bfloat16 [28672, 14336], P('mp', 'dp'), may hold values from -0.03125 to 0.03125
- in_basis: bfloat16 [8192, 8192], P('dp', 'mp'), may hold values from -0.0625 to 0.0625
- query_out: bfloat16 [128, 28672], P('dp', 'mp'), may hold values from -2.390625 to 2.390625
- query_in: bfloat16 [128, 8192], P('mp', 'dp'), may hold values from -2.390625 to 2.390625
- damping: float32 [1], replicated, may hold values from 0.5 to 2
Outputs:
- eigenvalues: float32 [14336, 8192], P('dp', 'mp')
- preconditioned: bfloat16 [4, 14336, 8192], P(None, 'dp', 'mp')
The draws below stay inside these ranges and needn't reach their ends.
All inputs are finite; a program needn't handle non-finite values.
Results may differ from the reference program's by a relative error of at most 0.033.
Values may be sent and summed in bfloat16 or wider, within the bound.
No kernel may reach another device: no remote copies, remote signals or barrier semaphores. Data moves between devices by JAX's collectives and lax.ppermute only.
A program may use at most 128 MiB of HBM per device.

```python
import math
import jax
import jax.numpy as jnp
from jax import lax

DI = 8192
DO = 28672
KG = 14336
Q = 4
RANK = 32
TOKENS = 512
SEQ = 256
N_DP = 4
N_MP = 8


def shard_levels(own_key, extent, shards, smallest, top_value):
    factor_of, own = 1.0, jax.random.fold_in(own_key, 6)
    for axis_at, shards_of in shards:
        draws = jnp.exp(jax.random.uniform(jax.random.fold_in(own, axis_at), (shards_of,), jnp.float32, smallest / len(shards), top_value / len(shards)))
        factor_of = factor_of * jnp.repeat(draws, extent[axis_at] // shards_of).reshape([-1 if axis == axis_at else 1 for axis in range(len(extent))])
    return factor_of


def normal_values(key, dims, spread, bound, cuts=(), kind=jnp.bfloat16):
    drawn = jax.random.normal(key, dims, jnp.float32) * spread
    if len(cuts) > 0:
        drawn = shard_levels(key, dims, cuts, -0.22, 0.18) * drawn
    return jnp.clip(drawn, min=-bound, max=bound).astype(kind)


def setup_inputs(seed: int = 0) -> dict:
    seeds = jax.random.split(jax.random.key(seed), 8)
    return {
        "out_grads": normal_values(seeds[0], (TOKENS, DO), 1.0, 6.0, ((0, 4), (1, 8))),
        "inputs": normal_values(seeds[1], (TOKENS, DI), 1.0, 6.0, ((0, 8), (1, 4))),
        "out_basis": normal_values(seeds[2], (DO, KG), DO ** -0.5, 0.03125, ((0, 8), (1, 4))),
        "in_basis": normal_values(seeds[3], (DI, DI), DI ** -0.5, 0.0625, ((0, 4), (1, 8))),
        "query_out": normal_values(seeds[4], (Q * RANK, DO), 0.4, 2.390625, ((0, 4), (1, 8))),
        "query_in": normal_values(seeds[5], (Q * RANK, DI), 0.4, 2.390625, ((0, 8), (1, 4))),
        "damping": jnp.clip(jnp.exp(jax.random.uniform(seeds[6], (1,), jnp.float32, math.log(0.5), math.log(2.0))), 0.5, 2.0),
    }


def blocked_product(rows, basis, parts):
    width = rows.shape[1] // parts

    def step(total, index):
        piece = lax.dynamic_slice_in_dim(rows, index * width, width, 1)
        block = lax.dynamic_slice_in_dim(basis, index * width, width, 0)
        term = jnp.dot(piece, block, preferred_element_type=jnp.float32).astype(jnp.bfloat16)
        term = lax.optimization_barrier(term)
        return total + term.astype(jnp.float32), None

    start = jnp.zeros((rows.shape[0], basis.shape[1]), jnp.float32)
    total, _ = lax.scan(step, start, jnp.arange(parts, dtype=jnp.int32))
    return total.astype(jnp.bfloat16)


def reference(out_grads, inputs, out_basis, in_basis, query_out, query_in, damping):
    rot_grads = blocked_product(out_grads, out_basis, N_MP)
    rot_left = blocked_product(query_out, out_basis, N_MP)
    rot_inputs = blocked_product(inputs, in_basis, N_DP)
    rot_right = blocked_product(query_in, in_basis, N_DP)
    squares = jnp.zeros((KG, DI), jnp.float32)
    for seq_index in range(2):
        grad_seq = rot_grads[seq_index * SEQ:(seq_index + 1) * SEQ]
        input_seq = rot_inputs[seq_index * SEQ:(seq_index + 1) * SEQ]
        rotated = jnp.dot(grad_seq.T, input_seq, preferred_element_type=jnp.float32)
        squares = squares + rotated * rotated
    eigenvalues = squares / (2.0 * SEQ)
    shifted = eigenvalues + damping[0]

    def one_query(index):
        left = lax.dynamic_slice_in_dim(rot_left, index * RANK, RANK, 0)
        right = lax.dynamic_slice_in_dim(rot_right, index * RANK, RANK, 0)
        product = jnp.dot(left.T, right, preferred_element_type=jnp.float32)
        return (product / shifted).astype(jnp.bfloat16)

    preconditioned = lax.map(one_query, jnp.arange(Q, dtype=jnp.int32))
    return eigenvalues, preconditioned
```

```python
import jax
import jax.numpy as jnp
from jax import lax
from jax.experimental import pallas as pl
from jax.experimental.pallas import tpu as pltpu
from jax.sharding import PartitionSpec as P

RANK = 32
QUARTERS = 4
HALVES = 2
PIECES = QUARTERS * HALVES
MIB = 1 << 20


def contract_rows(left, right):
    return lax.dot_general(
        left, right, (((0,), (0,)), ((), ())), preferred_element_type=jnp.float32
    )


def correct_kernel(tokens, damping_ref, rot_ref, act_ref, eig_ref, pre_ref):
    piece = rot_ref.shape[0] // PIECES
    per_seq = PIECES // 2

    def rows(ref, pieces, start, stop):
        return jnp.concatenate(
            [ref[p * piece + start:p * piece + stop, :] for p in pieces], axis=0
        )

    total = None
    for seq in range(2):
        pieces = range(seq * per_seq, (seq + 1) * per_seq)
        rotated = contract_rows(
            rows(rot_ref, pieces, 0, tokens), rows(act_ref, pieces, 0, tokens)
        )
        square = rotated * rotated
        total = square if total is None else total + square
    eig = total * (1.0 / (PIECES * tokens))
    eig_ref[...] = eig
    inverse = 1.0 / (eig + damping_ref[0])
    for quarter in range(QUARTERS):
        pieces = range(quarter * HALVES, (quarter + 1) * HALVES)
        product = contract_rows(
            rows(rot_ref, pieces, tokens, piece), rows(act_ref, pieces, tokens, piece)
        )
        pre_ref[quarter] = (product * inverse).astype(pre_ref.dtype)


def correct(tokens, damping, rot, act, tile):
    rows, outs = rot.shape
    ins = act.shape[1]
    tile = min(tile, outs)
    return pl.pallas_call(
        lambda *refs: correct_kernel(tokens, *refs),
        grid=(outs // tile,),
        in_specs=[
            pl.BlockSpec(memory_space=pltpu.SMEM),
            pl.BlockSpec((rows, tile), lambda i: (0, i)),
            pl.BlockSpec((rows, ins), lambda i: (0, 0)),
        ],
        out_specs=[
            pl.BlockSpec((tile, ins), lambda i: (i, 0)),
            pl.BlockSpec((QUARTERS, tile, ins), lambda i: (0, i, 0)),
        ],
        out_shape=[
            jax.ShapeDtypeStruct((outs, ins), jnp.float32),
            jax.ShapeDtypeStruct((QUARTERS, outs, ins), jnp.bfloat16),
        ],
        compiler_params=pltpu.CompilerParams(vmem_limit_bytes=40 * MIB),
        cost_estimate=pl.CostEstimate(
            flops=2 * rows * outs * ins, bytes_accessed=12 * outs * ins, transcendentals=0
        ),
        name="correct",
    )(damping, rot, act)


def by_pieces(blocks, tokens):
    holders, rows, width = blocks.shape
    if holders != PIECES:
        blocks = jnp.concatenate(
            [
                blocks[:, :tokens].reshape(PIECES, -1, width),
                blocks[:, tokens:].reshape(PIECES, -1, width),
            ],
            axis=1,
        )
    return blocks.reshape(-1, width)


def halved(tokens, queries):
    width = tokens.shape[1]
    return jnp.concatenate(
        [tokens.reshape(HALVES, -1, width), queries.reshape(HALVES, -1, width)], axis=1
    )


def shards(out_grads, inputs, out_basis, in_basis, query_out, query_in, damping):
    dp, mp = lax.axis_size("dp"), lax.axis_size("mp")
    tokens = out_grads.shape[0] * dp // PIECES
    act_rows = lax.all_gather(jnp.concatenate([inputs, query_in], axis=0), "mp", axis=0)
    act_rows = by_pieces(act_rows, inputs.shape[0])
    own = halved(out_grads, query_out)
    grad_rows = lax.all_gather(own, "dp", axis=0, tiled=True)
    grad_rows = by_pieces(grad_rows, out_grads.shape[0] // HALVES)
    terms = jnp.dot(grad_rows, out_basis, preferred_element_type=jnp.float32)
    part = lax.psum_scatter(
        terms.astype(jnp.bfloat16), "mp", scatter_dimension=0, tiled=True
    )
    rot = lax.all_gather(part, "mp", axis=0, tiled=True)
    act_terms = jnp.dot(act_rows, in_basis, preferred_element_type=jnp.float32)
    act = lax.psum(act_terms.astype(jnp.bfloat16), "dp")
    return tuple(correct(tokens, damping, rot, act, 256))


def solution(mesh):
    placed = (
        P("dp", "mp"),
        P("mp", "dp"),
        P("mp", "dp"),
        P("dp", "mp"),
        P("dp", "mp"),
        P("mp", "dp"),
        P(),
    )
    return jax.shard_map(
        shards,
        mesh=mesh,
        in_specs=placed,
        out_specs=(P("dp", "mp"), P(None, "dp", "mp")),
        check_vma=False,
    )
```

```python
import jax
import jax.numpy as jnp
from jax import lax
from jax.experimental import pallas as pl
from jax.experimental.pallas import tpu as pltpu
from jax.sharding import PartitionSpec as P

QUARTERS = 4
HALVES = 2
PIECES = QUARTERS * HALVES
MIB = 1 << 20
LANES = 128


def tile_of(width, limit):
    return max(t for t in range(LANES, limit + 1, LANES) if width % t == 0)


def contract_rows(left, right):
    return lax.dot_general(
        left, right, (((0,), (0,)), ((), ())), preferred_element_type=jnp.float32
    )


def add_rounded(left, right):
    return (left.astype(jnp.float32) + right.astype(jnp.float32)).astype(left.dtype)


def swap_quarter(x, bits):
    size = lax.axis_size("dp")
    step = bits * (size // QUARTERS)
    return lax.ppermute(x, "dp", [(i, i ^ step) for i in range(size)])


def swap_core(x):
    size = lax.axis_size("mp")
    return lax.ppermute(x, "mp", [(i, i ^ 1) for i in range(size)])


def move_chip(x, pairs):
    return lax.ppermute(
        x, "mp", [(HALVES * a + c, HALVES * b + c) for a, b in pairs for c in range(HALVES)]
    )


def line_sum(x):
    chips = lax.axis_size("mp") // HALVES
    last, inner = chips - 1, chips // 2
    chip = lax.axis_index("mp") // HALVES
    depth = jnp.minimum(chip, last - chip)
    for s in range(inner - 1):
        x = add_rounded(x, move_chip(x, [(s, s + 1), (last - s, last - s - 1)]))
    x = add_rounded(x, move_chip(x, [(inner - 1, inner), (inner, inner - 1)]))
    for s in range(inner - 1, 0, -1):
        came = move_chip(x, [(s, s - 1), (last - s, last - s + 1)])
        x = jnp.where(depth == s - 1, came, x)
    return x


def multiply_kernel(place_ref, low_ref, high_ref, basis_ref, keep_ref, send_ref, rows_ref):
    half = low_ref.shape[0]

    @pl.when(pl.program_id(0) == 0)
    def _():
        core = place_ref[1]
        rows_ref[pl.ds(pl.multiple_of(core * half, 16), half), :] = low_ref[...]
        rows_ref[pl.ds(pl.multiple_of((1 - core) * half, 16), half), :] = high_ref[...]

    terms = jnp.dot(rows_ref[...], basis_ref[...], preferred_element_type=jnp.float32)
    terms = terms.astype(keep_ref.dtype)
    keep_ref[...] = terms[:half]
    send_ref[...] = terms[half:]


def multiply(place, low, high, basis):
    half, depth = low.shape
    width = basis.shape[1]
    tile = tile_of(width, 512)
    rows = pl.BlockSpec((half, depth), lambda i: (0, 0))
    out = pl.BlockSpec((half, tile), lambda i: (0, i))
    return pl.pallas_call(
        multiply_kernel,
        grid=(width // tile,),
        in_specs=[
            pl.BlockSpec(memory_space=pltpu.SMEM),
            rows,
            rows,
            pl.BlockSpec((depth, tile), lambda i: (0, i)),
        ],
        out_specs=[out, out],
        out_shape=[jax.ShapeDtypeStruct((half, width), low.dtype)] * 2,
        scratch_shapes=[pltpu.VMEM((HALVES * half, depth), low.dtype)],
        compiler_params=pltpu.CompilerParams(vmem_limit_bytes=32 * MIB),
        cost_estimate=pl.CostEstimate(
            flops=4 * half * depth * width,
            bytes_accessed=2 * depth * width,
            transcendentals=0,
        ),
        name="multiply",
    )(place, low, high, basis)


def rotated_places(core):
    return [(0, core), (2 - core, core), (1 + core, core), (3, core)]


def correct_kernel(tokens, place_ref, damping_ref, *refs):
    groups = 2 * QUARTERS
    rot_refs, act_refs = refs[:groups], refs[groups:groups + HALVES]
    eig_ref, pre_ref, rot_tok, rot_qry, act_tok, act_qry = refs[groups + HALVES:]
    queries = rot_refs[0].shape[0] - tokens
    quarter, core = place_ref[0], place_ref[1]

    def put(tok, qry, piece, values):
        tok[pl.ds(pl.multiple_of(piece * tokens, 16), tokens), :] = values[:tokens]
        qry[pl.ds(pl.multiple_of(piece * queries, 16), queries), :] = values[tokens:]

    @pl.when(pl.program_id(0) == 0)
    def _():
        per_ref = PIECES // HALVES
        size = tokens + queries
        for piece in range(PIECES):
            at = piece % per_ref * size
            put(act_tok, act_qry, piece, act_refs[piece // per_ref][at:at + size, :])

    for held, refs_held in ((core, rot_refs[:QUARTERS]), (1 - core, rot_refs[QUARTERS:])):
        for (bits, half), ref in zip(rotated_places(held), refs_held):
            put(rot_tok, rot_qry, (quarter ^ bits) * HALVES + half, ref[...])

    length = tokens * PIECES // 2
    total = None
    for seq in range(2):
        rows = slice(seq * length, (seq + 1) * length)
        rotated = contract_rows(rot_tok[rows, :], act_tok[rows, :])
        square = rotated * rotated
        total = square if total is None else total + square
    eig = total * (1.0 / (2 * length))
    eig_ref[...] = eig
    inverse = 1.0 / (eig + damping_ref[0])
    rank = queries * HALVES
    for query in range(QUARTERS):
        rows = slice(query * rank, (query + 1) * rank)
        product = contract_rows(rot_qry[rows, :], act_qry[rows, :])
        pre_ref[query] = (product * inverse).astype(pre_ref.dtype)


def correct(tokens, place, damping, rot, act):
    size, outs = rot[0].shape
    rows, ins = act[0].shape
    queries = size - tokens
    tile = tile_of(outs, 256)
    smem = pl.BlockSpec(memory_space=pltpu.SMEM)
    dtype = rot[0].dtype
    return pl.pallas_call(
        lambda *refs: correct_kernel(tokens, *refs),
        grid=(outs // tile,),
        in_specs=[smem, smem]
        + [pl.BlockSpec((size, tile), lambda i: (0, i))] * len(rot)
        + [pl.BlockSpec((rows, ins), lambda i: (0, 0))] * len(act),
        out_specs=[
            pl.BlockSpec((tile, ins), lambda i: (i, 0)),
            pl.BlockSpec((QUARTERS, tile, ins), lambda i: (0, i, 0)),
        ],
        out_shape=[
            jax.ShapeDtypeStruct((outs, ins), jnp.float32),
            jax.ShapeDtypeStruct((QUARTERS, outs, ins), dtype),
        ],
        scratch_shapes=[
            pltpu.VMEM((PIECES * tokens, tile), dtype),
            pltpu.VMEM((PIECES * queries, tile), dtype),
            pltpu.VMEM((PIECES * tokens, ins), dtype),
            pltpu.VMEM((PIECES * queries, ins), dtype),
        ],
        compiler_params=pltpu.CompilerParams(vmem_limit_bytes=40 * MIB),
        cost_estimate=pl.CostEstimate(
            flops=2 * PIECES * size * outs * ins,
            bytes_accessed=12 * outs * ins,
            transcendentals=0,
        ),
        name="correct",
    )(place, damping, *rot, *act)


def outer_rows(tokens, queries):
    size = lax.axis_size("dp")
    index = lax.axis_index("dp")
    step = 1
    while step < size // QUARTERS:
        pairs = [(i, i ^ step) for i in range(size)]
        first = (index // step) % 2 == 0

        def joined(x):
            other = lax.ppermute(x, "dp", pairs)
            return jnp.where(
                first, jnp.concatenate([x, other]), jnp.concatenate([other, x])
            )

        tokens, queries = joined(tokens), joined(queries)
        step *= 2
    return tokens, queries


def quarter_sum(low, high):
    size = lax.axis_size("dp")
    for bits in (1, 2):
        low = add_rounded(low, swap_quarter(low, bits))
        high = add_rounded(high, swap_quarter(high, 3 - bits))
    step = 1
    while step < size // QUARTERS:
        pairs = [(i, i ^ step) for i in range(size)]
        low = add_rounded(low, lax.ppermute(low, "dp", pairs))
        high = add_rounded(high, lax.ppermute(high, "dp", pairs))
        step *= 2
    return low, high


def activation_rows(inputs, query_in):
    tokens = inputs.shape[0]
    blocks = lax.all_gather(jnp.concatenate([inputs, query_in]), "mp", axis=0)
    holders, _, width = blocks.shape
    if holders != PIECES:
        blocks = jnp.concatenate(
            [
                blocks[:, :tokens].reshape(PIECES, -1, width),
                blocks[:, tokens:].reshape(PIECES, -1, width),
            ],
            axis=1,
        )
    return blocks.reshape(-1, width)


def shards(out_grads, inputs, out_basis, in_basis, query_out, query_in, damping):
    dp = lax.axis_size("dp")
    place = jnp.stack(
        [lax.axis_index("dp") // (dp // QUARTERS), lax.axis_index("mp") % HALVES]
    ).astype(jnp.int32)

    act_rows = activation_rows(inputs, query_in)

    tokens, queries = outer_rows(out_grads, query_out)
    length = tokens.shape[0] // HALVES
    rank = queries.shape[0] // HALVES
    own = [
        jnp.concatenate(
            [tokens[h * length:(h + 1) * length], queries[h * rank:(h + 1) * rank]]
        )
        for h in range(HALVES)
    ]
    beside = [swap_quarter(own[0], 2), swap_quarter(own[1], 1)]
    behind = [swap_quarter(own[0], 1), swap_quarter(own[1], 2)]
    across = [swap_quarter(beside[0], 1), swap_quarter(beside[1], 2)]

    held, handed = [], []
    for low, high in (own, beside, behind, across):
        keep, send = multiply(place, low, high, out_basis)
        total = line_sum(add_rounded(keep, swap_core(send)))
        held.append(total)
        handed.append(swap_core(total))

    act_terms = jnp.dot(act_rows, in_basis, preferred_element_type=jnp.float32)
    act_terms = act_terms.astype(jnp.bfloat16)
    cut = act_terms.shape[0] // HALVES
    act = quarter_sum(act_terms[:cut], act_terms[cut:])
    return tuple(correct(length, place, damping, held + handed, act))


def solution(mesh):
    placed = (
        P("dp", "mp"),
        P("mp", "dp"),
        P("mp", "dp"),
        P("dp", "mp"),
        P("dp", "mp"),
        P("mp", "dp"),
        P(),
    )
    return jax.shard_map(
        shards,
        mesh=mesh,
        in_specs=placed,
        out_specs=(P("dp", "mp"), P(None, "dp", "mp")),
        check_vma=False,
    )
```

```python
import jax
import jax.numpy as jnp
from jax import lax
from jax.experimental import pallas as pl
from jax.experimental.pallas import tpu as pltpu
from jax.sharding import PartitionSpec as P

QUARTERS = 4
HALVES = 2
PIECES = QUARTERS * HALVES
MIB = 1 << 20
LANES = 128
DEPTHS = 2


def tile_of(width, limit):
    return max(t for t in range(LANES, limit + 1, LANES) if width % t == 0)


def contract_rows(left, right):
    return lax.dot_general(
        left, right, (((0,), (0,)), ((), ())), preferred_element_type=jnp.float32
    )


def add_rounded(left, right):
    return (left.astype(jnp.float32) + right.astype(jnp.float32)).astype(left.dtype)


class Order:
    def __init__(self):
        self.token = None

    def call(
        self, kernel, operands, out_shape, in_specs=None, out_specs=None, unread=(),
        vmem=6 * MIB, **options,
    ):
        out_shape = list(out_shape)
        whole = pl.BlockSpec(memory_space=pltpu.VMEM)
        anywhere = pl.BlockSpec(memory_space=pl.ANY)
        in_specs = [whole] * len(operands) if in_specs is None else list(in_specs)
        out_specs = [whole] * len(out_shape) if out_specs is None else list(out_specs)
        given, made = len(operands), len(out_shape)
        tokens = [*unread] if self.token is None else [*unread, self.token]

        def body(*refs):
            start = given + len(tokens)
            kernel(*refs[:given], *refs[start:start + made], *refs[start + made + 1:])

        *results, self.token = pl.pallas_call(
            body,
            in_specs=in_specs + [anywhere] * len(tokens),
            out_specs=out_specs + [anywhere],
            out_shape=out_shape + [jax.ShapeDtypeStruct((8, LANES), jnp.float32)],
            compiler_params=pltpu.CompilerParams(vmem_limit_bytes=vmem),
            **options,
        )(*operands, *tokens)
        return results

    def add(self, *pairs, unread=()):
        count = len(pairs)

        def kernel(*refs):
            for i in range(count):
                refs[2 * count + i][...] = add_rounded(refs[2 * i][...], refs[2 * i + 1][...])

        shapes = [jax.ShapeDtypeStruct(x.shape, x.dtype) for x, _ in pairs]
        operands = [x for pair in pairs for x in pair]
        return self.call(kernel, operands, shapes, unread=unread, name="add")

    def pick(self, place, index, first, second):
        def kernel(place_ref, first_ref, second_ref, out_ref):
            @pl.when(place_ref[index] == 0)
            def _():
                out_ref[...] = first_ref[...]

            @pl.when(place_ref[index] != 0)
            def _():
                out_ref[...] = second_ref[...]

        vmem = pl.BlockSpec(memory_space=pltpu.VMEM)
        shape = jax.ShapeDtypeStruct(first.shape, first.dtype)
        in_specs = [pl.BlockSpec(memory_space=pltpu.SMEM), vmem, vmem]
        return self.call(kernel, [place, first, second], [shape], in_specs, name="pick")[0]


def swap_quarter(x, bits):
    size = lax.axis_size("dp")
    step = bits * (size // QUARTERS)
    return lax.ppermute(x, "dp", [(i, i ^ step) for i in range(size)])


def swap_core(x):
    size = lax.axis_size("mp")
    return lax.ppermute(x, "mp", [(i, i ^ 1) for i in range(size)])


def move_chip(x, pairs):
    return lax.ppermute(
        x, "mp", [(HALVES * a + c, HALVES * b + c) for a, b in pairs for c in range(HALVES)]
    )


class LineSum:
    def __init__(self, x):
        chips = lax.axis_size("mp") // HALVES
        last, inner = chips - 1, chips // 2
        self.inward = [[(s, s + 1), (last - s, last - s - 1)] for s in range(inner - 1)]
        self.inward.append([(inner - 1, inner), (inner, inner - 1)])
        self.outward = [
            (s, [(s, s - 1), (last - s, last - s + 1)]) for s in range(inner - 1, 0, -1)
        ]
        self.x, self.hop = x, 0
        self.came = move_chip(x, self.inward[0])

    def add(self, order):
        self.x, = order.add((self.x, self.came))
        self.hop += 1
        inward = self.hop < len(self.inward)
        self.came = move_chip(self.x, self.inward[self.hop] if inward else self.outward[0][1])
        return inward

    def spread(self, order, place):
        for at, (s, _) in enumerate(self.outward):
            self.x = order.pick(place, DEPTHS + s - 1, self.came, self.x)
            if at + 1 < len(self.outward):
                self.came = move_chip(self.x, self.outward[at + 1][1])
        return self.x


def join_rows(order, tokens, queries):
    length, rank = tokens.shape[0] // HALVES, queries.shape[0] // HALVES

    def kernel(tokens_ref, queries_ref, *half_refs):
        for h, ref in enumerate(half_refs):
            ref[:length] = tokens_ref[h * length:(h + 1) * length, :]
            ref[length:] = queries_ref[h * rank:(h + 1) * rank, :]

    shape = jax.ShapeDtypeStruct((length + rank, tokens.shape[1]), tokens.dtype)
    return order.call(kernel, [tokens, queries], [shape] * HALVES, name="join_rows")


def place_rows(place_ref, low_ref, high_ref, rows_ref):
    half = low_ref.shape[0]
    core = place_ref[1]
    rows_ref[pl.ds(pl.multiple_of(core * half, 16), half), :] = low_ref[...]
    rows_ref[pl.ds(pl.multiple_of((1 - core) * half, 16), half), :] = high_ref[...]


def multiply(order, place, low, high, basis, held, unread=()):
    half, depth = low.shape
    width = basis.shape[1]
    tile = tile_of(width, 512)
    first = held is None

    def product(rows_ref, basis_ref, keep_ref, send_ref, columns):
        terms = jnp.dot(
            rows_ref[...], basis_ref[:, columns], preferred_element_type=jnp.float32
        ).astype(keep_ref.dtype)
        keep_ref[:, columns] = terms[:half]
        send_ref[:, columns] = terms[half:]

    def load_kernel(
        place_ref, low_ref, high_ref, basis_ref,
        keep_ref, send_ref, low_out, high_out, held_ref, rows_ref, sems,
    ):
        copies = [
            pltpu.make_async_copy(
                basis_ref.at[:, pl.ds(at, tile)],
                held_ref.at[:, pl.ds(at, tile)],
                sems.at[at // tile],
            )
            for at in range(0, width, tile)
        ]
        for copy in copies:
            copy.start()
        place_rows(place_ref, low_ref, high_ref, rows_ref)
        low_out[...] = low_ref[...]
        high_out[...] = high_ref[...]
        for i, copy in enumerate(copies):
            copy.wait()
            product(rows_ref, held_ref, keep_ref, send_ref, pl.ds(i * tile, tile))

    def held_kernel(place_ref, low_ref, high_ref, held_ref, keep_ref, send_ref, rows_ref):
        place_rows(place_ref, low_ref, high_ref, rows_ref)

        @pl.loop(0, width // tile)
        def _(i):
            columns = pl.ds(pl.multiple_of(i * tile, tile), tile)
            product(rows_ref, held_ref, keep_ref, send_ref, columns)

    smem = pl.BlockSpec(memory_space=pltpu.SMEM)
    vmem = pl.BlockSpec(memory_space=pltpu.VMEM)
    anywhere = pl.BlockSpec(memory_space=pl.ANY)
    out = jax.ShapeDtypeStruct((half, width), low.dtype)
    row = jax.ShapeDtypeStruct((half, depth), low.dtype)
    scratch = [pltpu.VMEM((HALVES * half, depth), low.dtype)]
    if first:
        return order.call(
            load_kernel,
            [place, low, high, basis],
            [out, out, row, row, pltpu.VMEM(basis.shape, basis.dtype)],
            [smem, vmem, vmem, anywhere],
            scratch_shapes=scratch + [pltpu.SemaphoreType.DMA((width // tile,))],
                name="load_and_multiply",
        )
    held = pltpu.with_memory_space_constraint(held, pltpu.VMEM)
    return order.call(
        held_kernel,
        [place, low, high, held],
        [out, out],
        [smem, vmem, vmem, vmem],
        unread=unread,
        scratch_shapes=scratch,
        name="multiply",
    )


def multiply_activations(order, rows, basis, unread=()):
    count, depth = rows.shape
    width, half = basis.shape[1], rows.shape[0] // HALVES
    tile = tile_of(width, 256)

    def kernel(rows_ref, basis_ref, low_ref, high_ref):
        for h, ref in enumerate((low_ref, high_ref)):
            terms = jnp.dot(
                rows_ref[h * half:(h + 1) * half, :],
                basis_ref[...],
                preferred_element_type=jnp.float32,
            )
            ref[...] = terms.astype(ref.dtype)

    out = pl.BlockSpec((half, tile), lambda i: (0, i))
    return order.call(
        kernel,
        [rows, basis],
        [jax.ShapeDtypeStruct((half, width), rows.dtype)] * HALVES,
        [
            pl.BlockSpec((count, depth), lambda i: (0, 0)),
            pl.BlockSpec((depth, tile), lambda i: (0, i)),
        ],
        [out, out],
        unread=unread,
        grid=(width // tile,),
        name="multiply_activations",
    )


def rotated_places(core):
    return [(0, core), (2 - core, core), (1 + core, core), (3, core)]


def correct_kernel(tokens, place_ref, damping_ref, *refs):
    groups = 2 * QUARTERS
    rot_refs, act_refs = refs[:groups], refs[groups:groups + HALVES]
    eig_ref, pre_ref, rot_tok, rot_qry, act_tok, act_qry = refs[groups + HALVES:]
    queries = rot_refs[0].shape[0] - tokens
    quarter, core = place_ref[0], place_ref[1]

    def put(tok, qry, piece, values):
        tok[pl.ds(pl.multiple_of(piece * tokens, 16), tokens), :] = values[:tokens]
        qry[pl.ds(pl.multiple_of(piece * queries, 16), queries), :] = values[tokens:]

    @pl.when(pl.program_id(0) == 0)
    def _():
        per_ref = PIECES // HALVES
        size = tokens + queries
        for piece in range(PIECES):
            at = piece % per_ref * size
            put(act_tok, act_qry, piece, act_refs[piece // per_ref][at:at + size, :])

    for held, refs_held in ((core, rot_refs[:QUARTERS]), (1 - core, rot_refs[QUARTERS:])):
        for (bits, half), ref in zip(rotated_places(held), refs_held):
            put(rot_tok, rot_qry, (quarter ^ bits) * HALVES + half, ref[...])

    length = tokens * PIECES // 2
    total = None
    for seq in range(2):
        rows = slice(seq * length, (seq + 1) * length)
        rotated = contract_rows(rot_tok[rows, :], act_tok[rows, :])
        square = rotated * rotated
        total = square if total is None else total + square
    eig = total * (1.0 / (2 * length))
    eig_ref[...] = eig
    inverse = 1.0 / (eig + damping_ref[0])
    rank = queries * HALVES
    for query in range(QUARTERS):
        rows = slice(query * rank, (query + 1) * rank)
        product = contract_rows(rot_qry[rows, :], act_qry[rows, :])
        pre_ref[query] = (product * inverse).astype(pre_ref.dtype)


def correct(order, tokens, place, damping, rot, act):
    size, outs = rot[0].shape
    rows, ins = act[0].shape
    queries = size - tokens
    tile = tile_of(outs, 256)
    smem = pl.BlockSpec(memory_space=pltpu.SMEM)
    dtype = rot[0].dtype
    return order.call(
        lambda *refs: correct_kernel(tokens, *refs),
        [place, damping, *rot, *act],
        [
            jax.ShapeDtypeStruct((outs, ins), jnp.float32),
            jax.ShapeDtypeStruct((QUARTERS, outs, ins), dtype),
        ],
        [smem, smem]
        + [pl.BlockSpec((size, tile), lambda i: (0, i))] * len(rot)
        + [pl.BlockSpec((rows, ins), lambda i: (0, 0))] * len(act),
        [
            pl.BlockSpec((tile, ins), lambda i: (i, 0)),
            pl.BlockSpec((QUARTERS, tile, ins), lambda i: (0, i, 0)),
        ],
        grid=(outs // tile,),
        scratch_shapes=[
            pltpu.VMEM((PIECES * tokens, tile), dtype),
            pltpu.VMEM((PIECES * queries, tile), dtype),
            pltpu.VMEM((PIECES * tokens, ins), dtype),
            pltpu.VMEM((PIECES * queries, ins), dtype),
        ],
        vmem=32 * MIB,
        name="correct",
    )


def outer_rows(tokens, queries):
    size = lax.axis_size("dp")
    index = lax.axis_index("dp")
    step = 1
    while step < size // QUARTERS:
        pairs = [(i, i ^ step) for i in range(size)]
        first = (index // step) % 2 == 0

        def joined(x):
            other = lax.ppermute(x, "dp", pairs)
            return jnp.where(
                first, jnp.concatenate([x, other]), jnp.concatenate([other, x])
            )

        tokens, queries = joined(tokens), joined(queries)
        step *= 2
    return tokens, queries


class QuarterSum:
    def __init__(self, low, high):
        size = lax.axis_size("dp")
        outer = size // QUARTERS
        self.hops = [(outer, 2 * outer), (2 * outer, outer)]
        step = 1
        while step < outer:
            self.hops.append((step, step))
            step *= 2
        self.size, self.pair, self.hop = size, (low, high), 0
        self.send()

    def send(self):
        self.came = [
            lax.ppermute(x, "dp", [(i, i ^ step) for i in range(self.size)])
            for x, step in zip(self.pair, self.hops[self.hop])
        ]

    def add(self, order):
        self.pair = order.add(*zip(self.pair, self.came))
        self.hop += 1
        if self.hop < len(self.hops):
            self.send()


def activation_rows(inputs, query_in):
    tokens = inputs.shape[0]
    blocks = lax.all_gather(jnp.concatenate([inputs, query_in]), "mp", axis=0)
    holders, _, width = blocks.shape
    if holders != PIECES:
        blocks = jnp.concatenate(
            [
                blocks[:, :tokens].reshape(PIECES, -1, width),
                blocks[:, tokens:].reshape(PIECES, -1, width),
            ],
            axis=1,
        )
    return blocks.reshape(-1, width)


def place_of_device():
    dp, mp = lax.axis_size("dp"), lax.axis_size("mp")
    chips, chip = mp // HALVES, lax.axis_index("mp") // HALVES
    depth = jnp.minimum(chip, chips - 1 - chip)
    values = [lax.axis_index("dp") // (dp // QUARTERS), lax.axis_index("mp") % HALVES]
    values += [jnp.abs(depth - s) for s in range(chips // 2)]
    return jnp.stack(values).astype(jnp.int32)


def shards(out_grads, inputs, out_basis, in_basis, query_out, query_in, damping):
    order = Order()
    place = place_of_device()
    act_rows = activation_rows(inputs, query_in)
    tokens, queries = outer_rows(out_grads, query_out)
    length = tokens.shape[0] // HALVES

    own = join_rows(order, tokens, queries)
    beside = [swap_quarter(own[0], 2), swap_quarter(own[1], 1)]
    own_keep, own_send, *again, held = multiply(order, place, *own, out_basis, None)
    own_came = swap_core(own_send)
    behind = [swap_quarter(again[0], 1), swap_quarter(again[1], 2)]
    across = [swap_quarter(beside[0], 1), swap_quarter(beside[1], 2)]

    def rotate(pair, unread=()):
        keep, send = multiply(order, place, *pair, out_basis, held, unread)
        return keep, swap_core(send)

    def settle(total):
        total = total.spread(order, place)
        return total, swap_core(total)

    def start(keep, came, unread=()):
        return LineSum(order.add((keep, came), unread=unread)[0])

    def inward(line):
        while line.add(order):
            pass

    pair = rotate(beside)
    first = start(own_keep, own_came)
    second = start(*pair)
    pair = rotate(behind)
    first.add(order)
    third = start(*pair, unread=across)
    pair = rotate(across, [second.came])
    acts = QuarterSum(*multiply_activations(order, act_rows, in_basis, [first.came]))
    second.add(order)
    fourth = start(*pair)
    inward(first)
    third.add(order)
    inward(second)
    done = [settle(first)]
    acts.add(order)
    fourth.add(order)
    inward(third)
    done.append(settle(second))
    inward(fourth)
    while acts.hop < len(acts.hops):
        acts.add(order)
    done.append(settle(third))
    done.append(settle(fourth))

    rot = [total for total, _ in done] + [other for _, other in done]
    return tuple(correct(order, length, place, damping, rot, acts.pair))


def solution(mesh):
    placed = (
        P("dp", "mp"),
        P("mp", "dp"),
        P("mp", "dp"),
        P("dp", "mp"),
        P("dp", "mp"),
        P("mp", "dp"),
        P(),
    )
    return jax.shard_map(
        shards,
        mesh=mesh,
        in_specs=placed,
        out_specs=(P("dp", "mp"), P(None, "dp", "mp")),
        check_vma=False,
    )
```

```python
import jax
import jax.numpy as jnp
from jax import lax
from jax.experimental import pallas as pl
from jax.experimental.pallas import tpu as pltpu
from jax.sharding import PartitionSpec as P

QUARTERS = 4
HALVES = 2
PIECES = QUARTERS * HALVES
MIB = 1 << 20
LANES = 128
CHIP = 2


def tile_of(width, limit):
    return max(t for t in range(LANES, limit + 1, LANES) if width % t == 0)


def contract_rows(left, right):
    return lax.dot_general(
        left, right, (((0,), (0,)), ((), ())), preferred_element_type=jnp.float32
    )


def streams_of(width):
    return max(count for count in (1, 2) if width % (count * LANES) == 0)


def in_hbm(x):
    return pltpu.with_memory_space_constraint(x, pltpu.HBM)


def add_rounded(left, right):
    return (left.astype(jnp.float32) + right.astype(jnp.float32)).astype(left.dtype)


class Order:
    def __init__(self):
        self.token = None

    def call(
        self, kernel, operands, out_shape, in_specs=None, out_specs=None, unread=(),
        vmem=6 * MIB, **options,
    ):
        out_shape = list(out_shape)
        whole = pl.BlockSpec(memory_space=pltpu.VMEM)
        anywhere = pl.BlockSpec(memory_space=pl.ANY)
        in_specs = [whole] * len(operands) if in_specs is None else list(in_specs)
        out_specs = [whole] * len(out_shape) if out_specs is None else list(out_specs)
        given, made = len(operands), len(out_shape)
        tokens = [*unread] if self.token is None else [*unread, self.token]

        def body(*refs):
            start = given + len(tokens)
            kernel(*refs[:given], *refs[start:start + made], *refs[start + made + 1:])

        *results, self.token = pl.pallas_call(
            body,
            in_specs=in_specs + [anywhere] * len(tokens),
            out_specs=out_specs + [anywhere],
            out_shape=out_shape + [jax.ShapeDtypeStruct((8, LANES), jnp.float32)],
            compiler_params=pltpu.CompilerParams(vmem_limit_bytes=vmem),
            **options,
        )(*operands, *tokens)
        return results

    def add(self, *pairs, unread=()):
        count = len(pairs)

        def kernel(*refs):
            for i in range(count):
                refs[2 * count + i][...] = add_rounded(refs[2 * i][...], refs[2 * i + 1][...])

        shapes = [jax.ShapeDtypeStruct(x.shape, x.dtype) for x, _ in pairs]
        operands = [x for pair in pairs for x in pair]
        return self.call(kernel, operands, shapes, unread=unread, name="add")


def swap_quarter(x, bits):
    size = lax.axis_size("dp")
    step = bits * (size // QUARTERS)
    return lax.ppermute(x, "dp", [(i, i ^ step) for i in range(size)])


def swap_core(x):
    size = lax.axis_size("mp")
    return lax.ppermute(x, "mp", [(i, i ^ 1) for i in range(size)])


def move_chip(x, pairs):
    return lax.ppermute(
        x, "mp", [(HALVES * a + c, HALVES * b + c) for a, b in pairs for c in range(HALVES)]
    )


class LineSum:
    def __init__(self, place, count):
        self.place, self.count = place, count
        self.chips = lax.axis_size("mp") // HALVES
        self.deepest = self.chips // 2 - 1
        self.lag = 2 * self.deepest + 1
        self.step, self.own, self.sent, self.came = 0, [], [], None

    def pairs(self, right):
        found = []
        for chip in range(self.chips):
            depth = min(chip, self.chips - 1 - chip)
            inward = (chip < self.chips // 2) == right
            if not inward and depth == 0:
                continue
            age = depth if inward else self.lag - depth
            if 0 <= self.step - age < self.count:
                found.append((chip, chip + 1 if right else chip - 1))
        return found

    def advance(self, order, chunk, unread=()):
        deepest, chips = self.deepest, self.chips
        keep, other = chunk if chunk is not None else (None, None)
        operands = [self.place]
        own = list(self.own)
        if chunk is not None:
            operands += [keep, other]
        base = len(operands)
        history = (own[::-1] + [own[0] if own else keep] * deepest)[:deepest]
        some = keep if keep is not None else own[-1]
        sent = (self.sent[::-1] + [(some, some)] * max(deepest, 1))[:max(deepest, 1)]
        came = self.came if self.came is not None else (some, some)
        operands += history + [x for pair in sent for x in pair] + list(came)
        smem, whole = pl.BlockSpec(memory_space=pltpu.SMEM), pl.BlockSpec(memory_space=pltpu.VMEM)
        fresh = chunk is not None

        def kernel(*refs):
            place_ref, rest = refs[0], refs[base:]
            past = rest[:deepest]
            sents = rest[deepest:deepest + 2 * len(sent)]
            from_left, from_right = rest[deepest + 2 * len(sent):][:2]
            outs = rest[deepest + 2 * len(sent) + 2:]
            right_ref, left_ref, total_ref = outs[:3]
            if fresh:
                own_ref = outs[3]
                own_ref[...] = add_rounded(refs[1][...], refs[2][...])
            for chip in range(chips):
                depth, left_side = min(chip, chips - 1 - chip), chip < chips // 2
                outer, inner = (from_left, from_right) if left_side else (from_right, from_left)
                to_inner, to_outer = (right_ref, left_ref) if left_side else (left_ref, right_ref)
                side = 0 if left_side else 1

                @pl.when(place_ref[CHIP] == chip)
                def _(depth=depth, outer=outer, inner=inner, to_inner=to_inner,
                      to_outer=to_outer, side=side):
                    if depth == 0:
                        to_inner[...] = own_ref[...] if fresh else inner[...]
                    else:
                        to_inner[...] = add_rounded(past[depth - 1][...], outer[...])
                    if depth == deepest:
                        to_outer[...] = add_rounded(sents[side][...], inner[...])
                    else:
                        to_outer[...] = inner[...]
                    if depth == 0:
                        total_ref[...] = to_outer[...]
                    else:
                        total_ref[...] = sents[2 * (depth - 1) + 1 - side][...]

        shape = jax.ShapeDtypeStruct(some.shape, some.dtype)
        right, left, total, *mine = order.call(
            kernel, operands, [shape] * (4 if fresh else 3),
            [smem] + [whole] * (len(operands) - 1), unread=unread, name="line_step",
        )
        self.own = (own + (mine if fresh else own[-1:]))[-max(deepest, 1):]
        self.sent = (self.sent + [(right, left)])[-max(deepest, 1):]
        to_right, to_left = self.pairs(True), self.pairs(False)
        self.came = (
            move_chip(right, to_right) if to_right else right,
            move_chip(left, to_left) if to_left else left,
        )
        ready = self.step >= self.lag
        self.step += 1
        return total if ready else None


def join_rows(order, tokens, queries, act_tokens, act_queries):
    length, rank = tokens.shape[0] // HALVES, queries.shape[0] // HALVES
    act_length = act_tokens.shape[0]

    def kernel(
        tokens_ref, queries_ref, act_tokens_ref, act_queries_ref, low_ref, high_ref, act_ref, sems
    ):
        copies = []
        for h, ref in enumerate((low_ref, high_ref)):
            copies += [
                pltpu.make_async_copy(
                    tokens_ref.at[pl.ds(h * length, length)],
                    ref.at[pl.ds(0, length)],
                    sems.at[h, 0],
                ),
                pltpu.make_async_copy(
                    queries_ref.at[pl.ds(h * rank, rank)],
                    ref.at[pl.ds(length, rank)],
                    sems.at[h, 1],
                ),
            ]
        for copy in copies:
            copy.start()
        act_ref[:act_length] = act_tokens_ref[...]
        act_ref[act_length:] = act_queries_ref[...]
        for copy in copies:
            copy.wait()

    half = jax.ShapeDtypeStruct((length + rank, tokens.shape[1]), tokens.dtype)
    act = (act_length + act_queries.shape[0], act_tokens.shape[1])
    anywhere, whole = pl.BlockSpec(memory_space=pl.ANY), pl.BlockSpec(memory_space=pltpu.VMEM)
    return order.call(
        kernel,
        [in_hbm(tokens), in_hbm(queries), in_hbm(act_tokens), in_hbm(act_queries)],
        [half, half, jax.ShapeDtypeStruct(act, act_tokens.dtype)],
        [anywhere, anywhere, whole, whole],
        scratch_shapes=[pltpu.SemaphoreType.DMA((HALVES, 2))],
        name="join_rows",
    )


def place_rows(place_ref, low_ref, high_ref, rows_ref):
    half = low_ref.shape[0]
    core = place_ref[1]
    rows_ref[pl.ds(pl.multiple_of(core * half, 16), half), :] = low_ref[...]
    rows_ref[pl.ds(pl.multiple_of((1 - core) * half, 16), half), :] = high_ref[...]


def multiply(order, place, low, high, basis, held, unread=()):
    half, depth = low.shape
    width = basis.shape[1]
    first = held is None

    streams = streams_of(width)
    block = width // streams
    tile = tile_of(block, 512)

    def product(rows_ref, basis_ref, keep_ref, send_ref, start, at):
        terms = jnp.dot(
            rows_ref[...], basis_ref[:, pl.ds(at, tile)], preferred_element_type=jnp.float32
        ).astype(send_ref.dtype)
        columns = pl.ds(pl.multiple_of(at - start, tile), tile)
        keep_ref[:, columns] = terms[:half]
        send_ref[:, columns] = terms[half:]

    def load_kernel(place_ref, low_ref, high_ref, basis_ref, *refs):
        keep_refs, send_refs = refs[:streams], refs[streams:2 * streams]
        held_ref, rows_ref, sems = refs[2 * streams:]
        copies = [
            pltpu.make_async_copy(
                basis_ref.at[:, pl.ds(at, tile)],
                held_ref.at[:, pl.ds(at, tile)],
                sems.at[at // tile],
            )
            for at in range(0, width, tile)
        ]
        for copy in copies:
            copy.start()
        place_rows(place_ref, low_ref, high_ref, rows_ref)
        for i, copy in enumerate(copies):
            copy.wait()
            at = i * tile
            start = at // block * block
            b = at // block
            product(rows_ref, held_ref, keep_refs[b], send_refs[b], start, at)

    def held_kernel(place_ref, low_ref, high_ref, held_ref, *refs):
        keep_refs, send_refs, rows_ref = refs[:streams], refs[streams:2 * streams], refs[-1]
        place_rows(place_ref, low_ref, high_ref, rows_ref)
        for start, keep_ref, send_ref in zip(range(0, width, block), keep_refs, send_refs):

            @pl.loop(0, block // tile)
            def _(i, start=start, keep_ref=keep_ref, send_ref=send_ref):
                at = pl.multiple_of(start + i * tile, tile)
                product(rows_ref, held_ref, keep_ref, send_ref, start, at)

    smem = pl.BlockSpec(memory_space=pltpu.SMEM)
    whole = pl.BlockSpec(memory_space=pltpu.VMEM)
    anywhere = pl.BlockSpec(memory_space=pl.ANY)
    outs = [jax.ShapeDtypeStruct((half, block), low.dtype)] * (2 * streams)
    scratch = [pltpu.VMEM((HALVES * half, depth), low.dtype)]
    if first:
        return order.call(
            load_kernel,
            [place, low, high, basis],
            outs + [pltpu.VMEM(basis.shape, basis.dtype)],
            [smem, whole, whole, anywhere],
            scratch_shapes=scratch + [pltpu.SemaphoreType.DMA((width // tile,))],
            name="load_and_multiply",
        )
    held = pltpu.with_memory_space_constraint(held, pltpu.VMEM)
    return order.call(
        held_kernel,
        [place, low, high, held],
        outs,
        [smem, whole, whole, whole],
        unread=unread,
        scratch_shapes=scratch,
        name="multiply",
    )


def multiply_activations(order, rows, basis, unread=()):
    count, depth = rows.shape
    width, half = basis.shape[1], rows.shape[0] // HALVES
    tile = tile_of(width, 256)

    def kernel(rows_ref, basis_ref, low_ref, high_ref):
        for h, ref in enumerate((low_ref, high_ref)):
            terms = jnp.dot(
                rows_ref[h * half:(h + 1) * half, :],
                basis_ref[...],
                preferred_element_type=jnp.float32,
            )
            ref[...] = terms.astype(ref.dtype)

    out = pl.BlockSpec((half, tile), lambda i: (0, i))
    return order.call(
        kernel,
        [in_hbm(rows), in_hbm(basis)],
        [jax.ShapeDtypeStruct((half, width), rows.dtype)] * HALVES,
        [
            pl.BlockSpec((count, depth), lambda i: (0, 0)),
            pl.BlockSpec((depth, tile), lambda i: (0, i)),
        ],
        [out, out],
        unread=unread,
        grid=(width // tile,),
        name="multiply_activations",
    )


def rotated_places(core):
    return [(0, core), (2 - core, core), (1 + core, core), (3, core)]


def correct_kernel(tokens, place_ref, damping_ref, *refs):
    groups = 2 * QUARTERS
    rot_refs, act_refs = refs[:groups], refs[groups:groups + HALVES]
    eig_ref, pre_ref, rot_tok, rot_qry, act_tok, act_qry = refs[groups + HALVES:]
    queries = rot_refs[0].shape[0] - tokens
    quarter, core = place_ref[0], place_ref[1]

    def put(tok, qry, piece, values):
        tok[pl.ds(pl.multiple_of(piece * tokens, 16), tokens), :] = values[:tokens]
        qry[pl.ds(pl.multiple_of(piece * queries, 16), queries), :] = values[tokens:]

    @pl.when(pl.program_id(0) == 0)
    def _():
        per_ref = PIECES // HALVES
        size = tokens + queries
        for piece in range(PIECES):
            at = piece % per_ref * size
            put(act_tok, act_qry, piece, act_refs[piece // per_ref][at:at + size, :])

    for held, refs_held in ((core, rot_refs[:QUARTERS]), (1 - core, rot_refs[QUARTERS:])):
        for (bits, half), ref in zip(rotated_places(held), refs_held):
            put(rot_tok, rot_qry, (quarter ^ bits) * HALVES + half, ref[...])

    length = tokens * PIECES // 2
    total = None
    for seq in range(2):
        rows = slice(seq * length, (seq + 1) * length)
        rotated = contract_rows(rot_tok[rows, :], act_tok[rows, :])
        square = rotated * rotated
        total = square if total is None else total + square
    eig = total * (1.0 / (2 * length))
    eig_ref[...] = eig
    inverse = 1.0 / (eig + damping_ref[0])
    rank = queries * HALVES
    for query in range(QUARTERS):
        rows = slice(query * rank, (query + 1) * rank)
        product = contract_rows(rot_qry[rows, :], act_qry[rows, :])
        pre_ref[query] = (product * inverse).astype(pre_ref.dtype)


def correct(order, tokens, place, damping, rot, act, block, outs, made):
    size, width = rot[0].shape
    rows, ins = act[0].shape
    queries = size - tokens
    tile = tile_of(width, 256)
    steps = width // tile
    smem = pl.BlockSpec(memory_space=pltpu.SMEM)
    dtype = rot[0].dtype
    operands = [place, damping, *rot, *act]
    count, kept = len(operands), len(made)
    return order.call(
        lambda *refs: correct_kernel(tokens, *refs[:count], *refs[count + kept:]),
        operands + list(made),
        [
            jax.ShapeDtypeStruct((outs, ins), jnp.float32),
            jax.ShapeDtypeStruct((QUARTERS, outs, ins), dtype),
        ],
        [smem, smem]
        + [pl.BlockSpec((size, tile), lambda i: (0, i))] * len(rot)
        + [pl.BlockSpec((rows, ins), lambda i: (0, 0))] * len(act)
        + [pl.BlockSpec(memory_space=pl.ANY)] * kept,
        [
            pl.BlockSpec((tile, ins), lambda i: (block * steps + i, 0)),
            pl.BlockSpec((QUARTERS, tile, ins), lambda i: (0, block * steps + i, 0)),
        ],
        input_output_aliases={count + i: i for i in range(kept)},
        grid=(steps,),
        scratch_shapes=[
            pltpu.VMEM((PIECES * tokens, tile), dtype),
            pltpu.VMEM((PIECES * queries, tile), dtype),
            pltpu.VMEM((PIECES * tokens, ins), dtype),
            pltpu.VMEM((PIECES * queries, ins), dtype),
        ],
        vmem=32 * MIB,
        name="correct",
    )


def outer_rows(tokens, queries):
    size = lax.axis_size("dp")
    index = lax.axis_index("dp")
    step = 1
    while step < size // QUARTERS:
        pairs = [(i, i ^ step) for i in range(size)]
        first = (index // step) % 2 == 0

        def joined(x):
            other = lax.ppermute(x, "dp", pairs)
            return jnp.where(
                first, jnp.concatenate([x, other]), jnp.concatenate([other, x])
            )

        tokens, queries = joined(tokens), joined(queries)
        step *= 2
    return tokens, queries


class QuarterSum:
    def __init__(self, low, high):
        size = lax.axis_size("dp")
        outer = size // QUARTERS
        self.hops = [(outer, 2 * outer), (2 * outer, outer)]
        step = 1
        while step < outer:
            self.hops.append((step, step))
            step *= 2
        self.size, self.pair, self.hop = size, (low, high), 0
        self.send()

    def send(self):
        self.came = [
            lax.ppermute(x, "dp", [(i, i ^ step) for i in range(self.size)])
            for x, step in zip(self.pair, self.hops[self.hop])
        ]

    def add(self, order):
        self.pair = order.add(*zip(self.pair, self.came))
        self.hop += 1
        if self.hop < len(self.hops):
            self.send()


def activation_rows(rows, tokens):
    blocks = lax.all_gather(rows, "mp", axis=0)
    holders, _, width = blocks.shape
    if holders != PIECES:
        blocks = jnp.concatenate(
            [
                blocks[:, :tokens].reshape(PIECES, -1, width),
                blocks[:, tokens:].reshape(PIECES, -1, width),
            ],
            axis=1,
        )
    return blocks.reshape(-1, width)


def shards(out_grads, inputs, out_basis, in_basis, query_out, query_in, damping):
    order = Order()
    dp, mp = lax.axis_index("dp"), lax.axis_index("mp")
    place = jnp.stack(
        [dp // (lax.axis_size("dp") // QUARTERS), mp % HALVES, mp // HALVES]
    ).astype(jnp.int32)

    tokens, queries = outer_rows(out_grads, query_out)
    length = tokens.shape[0] // HALVES
    low, high, act_rows = join_rows(order, tokens, queries, inputs, query_in)
    beside = [swap_quarter(low, 2), swap_quarter(high, 1)]
    behind = [swap_quarter(low, 1), swap_quarter(high, 2)]
    across = [swap_quarter(beside[0], 1), swap_quarter(beside[1], 2)]
    act_rows = activation_rows(act_rows, inputs.shape[0])

    width = out_basis.shape[1]
    lines = [LineSum(place, QUARTERS) for _ in range(streams_of(width))]
    held, acts = None, None
    chunks, late = [], []
    totals, swapped = [[] for _ in lines], [[] for _ in lines]

    def rotate(pair, unread=()):
        nonlocal held
        results = multiply(order, place, *pair, out_basis, held, unread)
        held = results.pop() if held is None else held
        came = [swap_core(x) for x in results[len(lines):]]
        chunks.append(list(zip(results, came)))

    def advance(s, unread=()):
        if s >= len(lines):
            return
        line, pins = lines[s], [*unread, *late]
        late.clear()
        chunk = chunks[line.step][s] if line.step < QUARTERS else None
        total = line.advance(order, chunk, pins)
        if total is not None:
            totals[s].append(total)
            swapped[s].append(swap_core(total))
            late.append(swapped[s][-1])

    def activate(unread=()):
        nonlocal acts
        acts = QuarterSum(*multiply_activations(order, act_rows, in_basis, unread))

    rotate((low, high))
    advance(0, [*beside])
    rotate(beside)
    advance(1, [*behind])
    rotate(behind)
    advance(0)
    advance(1, [*across])
    activate()
    rotate(across)
    advance(0)
    advance(1)
    advance(0)
    acts.add(order)
    advance(1)
    advance(0)
    acts.add(order)
    advance(1)
    advance(0)
    advance(1)
    advance(0)
    advance(1)
    while acts.hop < len(acts.hops):
        acts.add(order)
    while len(totals[-1]) < QUARTERS:
        for s in range(len(lines)):
            advance(s)

    made = ()
    for s in range(len(lines)):
        rot = totals[s] + swapped[s]
        made = correct(order, length, place, damping, rot, acts.pair, s, width, made)
    return tuple(made)


def solution(mesh):
    placed = (
        P("dp", "mp"),
        P("mp", "dp"),
        P("mp", "dp"),
        P("dp", "mp"),
        P("dp", "mp"),
        P("mp", "dp"),
        P(),
    )
    return jax.shard_map(
        shards,
        mesh=mesh,
        in_specs=placed,
        out_specs=(P("dp", "mp"), P(None, "dp", "mp")),
        check_vma=False,
    )
```

```python
import jax
import jax.numpy as jnp
from jax import lax
from jax.experimental import pallas as pl
from jax.experimental.pallas import tpu as pltpu
from jax.sharding import PartitionSpec as P

QUARTERS = 4
HALVES = 2
PIECES = QUARTERS * HALVES
MIB = 1 << 20
LANES = 128
CHIP = 2


def tile_of(width, limit):
    return max(t for t in range(LANES, limit + 1, LANES) if width % t == 0)


def contract_rows(left, right):
    return lax.dot_general(
        left, right, (((0,), (0,)), ((), ())), preferred_element_type=jnp.float32
    )


def streams_of(width):
    return max(count for count in (1, 2) if width % (count * LANES) == 0)


def in_hbm(x):
    return pltpu.with_memory_space_constraint(x, pltpu.HBM)


def add_rounded(left, right):
    return (left.astype(jnp.float32) + right.astype(jnp.float32)).astype(left.dtype)


class Order:
    def __init__(self):
        self.token = None

    def call(
        self, kernel, operands, out_shape, in_specs=None, out_specs=None, unread=(),
        vmem=6 * MIB, **options,
    ):
        out_shape = list(out_shape)
        whole = pl.BlockSpec(memory_space=pltpu.VMEM)
        anywhere = pl.BlockSpec(memory_space=pl.ANY)
        in_specs = [whole] * len(operands) if in_specs is None else list(in_specs)
        out_specs = [whole] * len(out_shape) if out_specs is None else list(out_specs)
        given, made = len(operands), len(out_shape)
        tokens = [*unread] if self.token is None else [*unread, self.token]

        def body(*refs):
            start = given + len(tokens)
            kernel(*refs[:given], *refs[start:start + made], *refs[start + made + 1:])

        *results, self.token = pl.pallas_call(
            body,
            in_specs=in_specs + [anywhere] * len(tokens),
            out_specs=out_specs + [anywhere],
            out_shape=out_shape + [jax.ShapeDtypeStruct((8, LANES), jnp.float32)],
            compiler_params=pltpu.CompilerParams(vmem_limit_bytes=vmem),
            **options,
        )(*operands, *tokens)
        return results

    def add(self, *pairs, unread=()):
        count = len(pairs)

        def kernel(*refs):
            for i in range(count):
                refs[2 * count + i][...] = add_rounded(refs[2 * i][...], refs[2 * i + 1][...])

        shapes = [jax.ShapeDtypeStruct(x.shape, x.dtype) for x, _ in pairs]
        operands = [x for pair in pairs for x in pair]
        return self.call(kernel, operands, shapes, unread=unread, name="add")


def swap_quarter(x, bits):
    size = lax.axis_size("dp")
    step = bits * (size // QUARTERS)
    return lax.ppermute(x, "dp", [(i, i ^ step) for i in range(size)])


def swap_core(x):
    size = lax.axis_size("mp")
    return lax.ppermute(x, "mp", [(i, i ^ 1) for i in range(size)])


def move_chip(x, pairs):
    return lax.ppermute(
        x, "mp", [(HALVES * a + c, HALVES * b + c) for a, b in pairs for c in range(HALVES)]
    )


class LineSum:
    def __init__(self, place, count):
        self.place, self.count = place, count
        self.chips = lax.axis_size("mp") // HALVES
        self.deepest = self.chips // 2 - 1
        self.lag = 2 * self.deepest + 1
        self.step, self.own, self.sent, self.came = 0, [], [], None

    def swaps(self, odd):
        found = []
        for chip in range(odd, self.chips - 1, 2):
            depths = [min(c, self.chips - 1 - c) for c in (chip, chip + 1)]
            if depths[0] == depths[1]:
                ages = [depths[0]]
            else:
                ages = [min(depths), self.lag - max(depths)]
            if any(0 <= self.step - age < self.count for age in ages):
                found += [(chip, chip + 1), (chip + 1, chip)]
        return found

    def advance(self, order, chunk, unread=()):
        deepest, chips = self.deepest, self.chips
        keep, other = chunk if chunk is not None else (None, None)
        operands = [self.place]
        own = list(self.own)
        if chunk is not None:
            operands += [keep, other]
        base = len(operands)
        history = (own[::-1] + [own[0] if own else keep] * deepest)[:deepest]
        some = keep if keep is not None else own[-1]
        sent = (self.sent[::-1] + [(some, some)] * max(deepest, 1))[:max(deepest, 1)]
        came = self.came if self.came is not None else (some, some)
        operands += history + [x for pair in sent for x in pair] + list(came)
        smem, whole = pl.BlockSpec(memory_space=pltpu.SMEM), pl.BlockSpec(memory_space=pltpu.VMEM)
        fresh = chunk is not None

        def kernel(*refs):
            place_ref, rest = refs[0], refs[base:]
            past = rest[:deepest]
            sents = rest[deepest:deepest + 2 * len(sent)]
            even, odd = rest[deepest + 2 * len(sent):][:2]
            outs = rest[deepest + 2 * len(sent) + 2:]
            even_ref, odd_ref, total_ref = outs[:3]
            if fresh:
                own_ref = outs[3]
                own_ref[...] = add_rounded(refs[1][...], refs[2][...])
            for chip in range(chips):
                depth, left_side = min(chip, chips - 1 - chip), chip < chips // 2
                by_even = left_side == (chip % 2 == 0)
                outer, inner = (odd, even) if by_even else (even, odd)
                to_inner, to_outer = (even_ref, odd_ref) if by_even else (odd_ref, even_ref)
                side = 0 if by_even else 1

                @pl.when(place_ref[CHIP] == chip)
                def _(depth=depth, outer=outer, inner=inner, to_inner=to_inner,
                      to_outer=to_outer, side=side):
                    if depth == 0:
                        to_inner[...] = own_ref[...] if fresh else inner[...]
                    else:
                        to_inner[...] = add_rounded(past[depth - 1][...], outer[...])
                    if depth == deepest:
                        to_outer[...] = add_rounded(sents[side][...], inner[...])
                    else:
                        to_outer[...] = inner[...]
                    if depth == 0:
                        total_ref[...] = to_outer[...]
                    else:
                        total_ref[...] = sents[2 * (depth - 1) + 1 - side][...]

        shape = jax.ShapeDtypeStruct(some.shape, some.dtype)
        even, odd, total, *mine = order.call(
            kernel, operands, [shape] * (4 if fresh else 3),
            [smem] + [whole] * (len(operands) - 1), unread=unread, name="line_step",
        )
        self.own = (own + (mine if fresh else own[-1:]))[-max(deepest, 1):]
        self.sent = (self.sent + [(even, odd)])[-max(deepest, 1):]
        self.came = tuple(
            move_chip(x, swaps) if swaps else x
            for x, swaps in ((even, self.swaps(0)), (odd, self.swaps(1)))
        )
        ready = self.step >= self.lag
        self.step += 1
        return total if ready else None


def join_rows(order, tokens, queries, act_tokens, act_queries):
    length, rank = tokens.shape[0] // HALVES, queries.shape[0] // HALVES
    act_length = act_tokens.shape[0]

    def kernel(
        tokens_ref, queries_ref, act_tokens_ref, act_queries_ref, low_ref, high_ref, act_ref, sems
    ):
        copies = []
        for h, ref in enumerate((low_ref, high_ref)):
            copies += [
                pltpu.make_async_copy(
                    tokens_ref.at[pl.ds(h * length, length)],
                    ref.at[pl.ds(0, length)],
                    sems.at[h, 0],
                ),
                pltpu.make_async_copy(
                    queries_ref.at[pl.ds(h * rank, rank)],
                    ref.at[pl.ds(length, rank)],
                    sems.at[h, 1],
                ),
            ]
        copies.append(
            pltpu.make_async_copy(
                act_tokens_ref, act_ref.at[pl.ds(0, act_length)], sems.at[HALVES, 0]
            )
        )
        for copy in copies:
            copy.start()
        act_ref[act_length:] = act_queries_ref[...]
        for copy in copies:
            copy.wait()

    half = jax.ShapeDtypeStruct((length + rank, tokens.shape[1]), tokens.dtype)
    act = (act_length + act_queries.shape[0], act_tokens.shape[1])
    anywhere, whole = pl.BlockSpec(memory_space=pl.ANY), pl.BlockSpec(memory_space=pltpu.VMEM)
    return order.call(
        kernel,
        [in_hbm(tokens), in_hbm(queries), in_hbm(act_tokens), in_hbm(act_queries)],
        [half, half, jax.ShapeDtypeStruct(act, act_tokens.dtype)],
        [anywhere, anywhere, anywhere, whole],
        scratch_shapes=[pltpu.SemaphoreType.DMA((HALVES + 1, 2))],
        name="join_rows",
    )


def place_rows(place_ref, low_ref, high_ref, rows_ref):
    half = low_ref.shape[0]
    core = place_ref[1]
    rows_ref[pl.ds(pl.multiple_of(core * half, 16), half), :] = low_ref[...]
    rows_ref[pl.ds(pl.multiple_of((1 - core) * half, 16), half), :] = high_ref[...]


def multiply(order, place, low, high, basis, held, unread=()):
    half, depth = low.shape
    width = basis.shape[1]
    first = held is None

    streams = streams_of(width)
    block = width // streams
    tile = tile_of(width, 512)

    def product(rows_ref, basis_ref, keep_refs, send_refs, at):
        terms = jnp.dot(
            rows_ref[...], basis_ref[:, at:at + tile], preferred_element_type=jnp.float32
        ).astype(rows_ref.dtype)
        for b in range(streams):
            start, stop = max(at, b * block), min(at + tile, (b + 1) * block)
            if start < stop:
                columns = slice(start - b * block, stop - b * block)
                keep_refs[b][:, columns] = terms[:half, start - at:stop - at]
                send_refs[b][:, columns] = terms[half:, start - at:stop - at]

    def load_kernel(place_ref, low_ref, high_ref, basis_ref, *refs):
        keep_refs, send_refs = refs[:streams], refs[streams:2 * streams]
        held_ref, rows_ref, sems = refs[2 * streams:]
        copies = [
            pltpu.make_async_copy(
                basis_ref.at[:, pl.ds(at, tile)],
                held_ref.at[:, pl.ds(at, tile)],
                sems.at[at // tile],
            )
            for at in range(0, width, tile)
        ]
        for copy in copies:
            copy.start()
        place_rows(place_ref, low_ref, high_ref, rows_ref)
        for i, copy in enumerate(copies):
            copy.wait()
            product(rows_ref, held_ref, keep_refs, send_refs, i * tile)

    def held_kernel(place_ref, low_ref, high_ref, held_ref, *refs):
        keep_refs, send_refs, rows_ref = refs[:streams], refs[streams:2 * streams], refs[-1]
        place_rows(place_ref, low_ref, high_ref, rows_ref)
        for at in range(0, width, tile):
            product(rows_ref, held_ref, keep_refs, send_refs, at)

    smem = pl.BlockSpec(memory_space=pltpu.SMEM)
    whole = pl.BlockSpec(memory_space=pltpu.VMEM)
    anywhere = pl.BlockSpec(memory_space=pl.ANY)
    outs = [jax.ShapeDtypeStruct((half, block), low.dtype)] * (2 * streams)
    scratch = [pltpu.VMEM((HALVES * half, depth), low.dtype)]
    if first:
        return order.call(
            load_kernel,
            [place, low, high, basis],
            outs + [pltpu.VMEM(basis.shape, basis.dtype)],
            [smem, whole, whole, anywhere],
            scratch_shapes=scratch + [pltpu.SemaphoreType.DMA((width // tile,))],
            name="load_and_multiply",
        )
    held = pltpu.with_memory_space_constraint(held, pltpu.VMEM)
    return order.call(
        held_kernel,
        [place, low, high, held],
        outs,
        [smem, whole, whole, whole],
        unread=unread,
        scratch_shapes=scratch,
        name="multiply",
    )


def multiply_activations(order, rows, basis, unread=()):
    count, depth = rows.shape
    width, half = basis.shape[1], rows.shape[0] // HALVES
    tile = tile_of(width, 256)

    def kernel(rows_ref, basis_ref, low_ref, high_ref):
        for h, ref in enumerate((low_ref, high_ref)):
            terms = jnp.dot(
                rows_ref[h * half:(h + 1) * half, :],
                basis_ref[...],
                preferred_element_type=jnp.float32,
            )
            ref[...] = terms.astype(ref.dtype)

    out = pl.BlockSpec((half, tile), lambda i: (0, i))
    return order.call(
        kernel,
        [in_hbm(rows), in_hbm(basis)],
        [jax.ShapeDtypeStruct((half, width), rows.dtype)] * HALVES,
        [
            pl.BlockSpec((count, depth), lambda i: (0, 0)),
            pl.BlockSpec((depth, tile), lambda i: (0, i)),
        ],
        [out, out],
        unread=unread,
        grid=(width // tile,),
        name="multiply_activations",
    )


def rotated_places(core):
    return [(0, core), (2 - core, core), (1 + core, core), (3, core)]


def correct_kernel(tokens, place_ref, damping_ref, *refs):
    groups = 2 * QUARTERS
    rot_refs, act_refs = refs[:groups], refs[groups:groups + HALVES]
    eig_ref, pre_ref, rot_tok, rot_qry, act_tok, act_qry = refs[groups + HALVES:]
    queries = rot_refs[0].shape[0] - tokens
    quarter, core = place_ref[0], place_ref[1]

    def put(tok, qry, piece, values):
        tok[pl.ds(pl.multiple_of(piece * tokens, 16), tokens), :] = values[:tokens]
        qry[pl.ds(pl.multiple_of(piece * queries, 16), queries), :] = values[tokens:]

    @pl.when(pl.program_id(0) == 0)
    def _():
        per_ref = PIECES // HALVES
        size = tokens + queries
        for piece in range(PIECES):
            at = piece % per_ref * size
            put(act_tok, act_qry, piece, act_refs[piece // per_ref][at:at + size, :])

    for held, refs_held in ((core, rot_refs[:QUARTERS]), (1 - core, rot_refs[QUARTERS:])):
        for (bits, half), ref in zip(rotated_places(held), refs_held):
            put(rot_tok, rot_qry, (quarter ^ bits) * HALVES + half, ref[...])

    length = tokens * PIECES // 2
    total = None
    for seq in range(2):
        rows = slice(seq * length, (seq + 1) * length)
        rotated = contract_rows(rot_tok[rows, :], act_tok[rows, :])
        square = rotated * rotated
        total = square if total is None else total + square
    eig = total * (1.0 / (2 * length))
    eig_ref[...] = eig
    inverse = 1.0 / (eig + damping_ref[0])
    rank = queries * HALVES
    for query in range(QUARTERS):
        rows = slice(query * rank, (query + 1) * rank)
        product = contract_rows(rot_qry[rows, :], act_qry[rows, :])
        pre_ref[query] = (product * inverse).astype(pre_ref.dtype)


def correct(order, tokens, place, damping, rot, act, block, outs, made):
    size, width = rot[0].shape
    rows, ins = act[0].shape
    queries = size - tokens
    tile = tile_of(width, 256)
    steps = width // tile
    smem = pl.BlockSpec(memory_space=pltpu.SMEM)
    dtype = rot[0].dtype
    operands = [place, damping, *rot, *act]
    count, kept = len(operands), len(made)
    return order.call(
        lambda *refs: correct_kernel(tokens, *refs[:count], *refs[count + kept:]),
        operands + list(made),
        [
            jax.ShapeDtypeStruct((outs, ins), jnp.float32),
            jax.ShapeDtypeStruct((QUARTERS, outs, ins), dtype),
        ],
        [smem, smem]
        + [pl.BlockSpec((size, tile), lambda i: (0, i))] * len(rot)
        + [pl.BlockSpec((rows, ins), lambda i: (0, 0))] * len(act)
        + [pl.BlockSpec(memory_space=pl.ANY)] * kept,
        [
            pl.BlockSpec((tile, ins), lambda i: (block * steps + i, 0)),
            pl.BlockSpec((QUARTERS, tile, ins), lambda i: (0, block * steps + i, 0)),
        ],
        input_output_aliases={count + i: i for i in range(kept)},
        grid=(steps,),
        scratch_shapes=[
            pltpu.VMEM((PIECES * tokens, tile), dtype),
            pltpu.VMEM((PIECES * queries, tile), dtype),
            pltpu.VMEM((PIECES * tokens, ins), dtype),
            pltpu.VMEM((PIECES * queries, ins), dtype),
        ],
        vmem=32 * MIB,
        name="correct",
    )


def outer_rows(tokens, queries):
    size = lax.axis_size("dp")
    index = lax.axis_index("dp")
    step = 1
    while step < size // QUARTERS:
        pairs = [(i, i ^ step) for i in range(size)]
        first = (index // step) % 2 == 0

        def joined(x):
            other = lax.ppermute(x, "dp", pairs)
            return jnp.where(
                first, jnp.concatenate([x, other]), jnp.concatenate([other, x])
            )

        tokens, queries = joined(tokens), joined(queries)
        step *= 2
    return tokens, queries


class QuarterSum:
    def __init__(self, low, high):
        size = lax.axis_size("dp")
        outer = size // QUARTERS
        self.hops = [(outer, 2 * outer), (2 * outer, outer)]
        step = 1
        while step < outer:
            self.hops.append((step, step))
            step *= 2
        self.size, self.pair, self.hop = size, (low, high), 0
        self.send()

    def send(self):
        self.came = [
            lax.ppermute(x, "dp", [(i, i ^ step) for i in range(self.size)])
            for x, step in zip(self.pair, self.hops[self.hop])
        ]

    def add(self, order):
        self.pair = order.add(*zip(self.pair, self.came))
        self.hop += 1
        if self.hop < len(self.hops):
            self.send()


def activation_rows(rows, tokens):
    blocks = lax.all_gather(rows, "mp", axis=0)
    holders, _, width = blocks.shape
    if holders != PIECES:
        blocks = jnp.concatenate(
            [
                blocks[:, :tokens].reshape(PIECES, -1, width),
                blocks[:, tokens:].reshape(PIECES, -1, width),
            ],
            axis=1,
        )
    return blocks.reshape(-1, width)


def shards(out_grads, inputs, out_basis, in_basis, query_out, query_in, damping):
    order = Order()
    dp, mp = lax.axis_index("dp"), lax.axis_index("mp")
    place = jnp.stack(
        [dp // (lax.axis_size("dp") // QUARTERS), mp % HALVES, mp // HALVES]
    ).astype(jnp.int32)

    tokens, queries = outer_rows(out_grads, query_out)
    length = tokens.shape[0] // HALVES
    low, high, act_rows = join_rows(order, tokens, queries, inputs, query_in)
    beside = [swap_quarter(low, 2), swap_quarter(high, 1)]
    behind = [swap_quarter(low, 1), swap_quarter(high, 2)]
    across = [swap_quarter(beside[0], 1), swap_quarter(beside[1], 2)]
    act_rows = activation_rows(act_rows, inputs.shape[0])

    width = out_basis.shape[1]
    lines = [LineSum(place, QUARTERS) for _ in range(streams_of(width))]
    held, acts = None, None
    chunks, late = [], []
    totals, swapped = [[] for _ in lines], [[] for _ in lines]

    def rotate(pair, unread=()):
        nonlocal held
        results = multiply(order, place, *pair, out_basis, held, unread)
        held = results.pop() if held is None else held
        came = [swap_core(x) for x in results[len(lines):]]
        chunks.append(list(zip(results, came)))

    def advance(s, unread=()):
        if s >= len(lines):
            return
        line, pins = lines[s], [*unread, *late]
        late.clear()
        chunk = chunks[line.step][s] if line.step < QUARTERS else None
        total = line.advance(order, chunk, pins)
        if total is not None:
            totals[s].append(total)
            swapped[s].append(swap_core(total))
            late.append(swapped[s][-1])

    def activate(unread=()):
        nonlocal acts
        acts = QuarterSum(*multiply_activations(order, act_rows, in_basis, unread))

    rotate((low, high))
    advance(0)
    advance(1)
    rotate(beside)
    advance(0)
    rotate(behind, [*behind])
    advance(1)
    rotate(across, [*across])
    advance(0)
    advance(1)
    activate()
    advance(0)
    advance(1)
    advance(0)
    acts.add(order)
    advance(1)
    advance(0)
    acts.add(order)
    advance(1)
    advance(0)
    advance(1)
    while acts.hop < len(acts.hops):
        acts.add(order)
    while len(totals[-1]) < QUARTERS:
        for s in range(len(lines)):
            advance(s)

    made = ()
    for s in range(len(lines)):
        rot = totals[s] + swapped[s]
        made = correct(order, length, place, damping, rot, acts.pair, s, width, made)
    return tuple(made)


def solution(mesh):
    placed = (
        P("dp", "mp"),
        P("mp", "dp"),
        P("mp", "dp"),
        P("dp", "mp"),
        P("dp", "mp"),
        P("mp", "dp"),
        P(),
    )
    return jax.shard_map(
        shards,
        mesh=mesh,
        in_specs=placed,
        out_specs=(P("dp", "mp"), P(None, "dp", "mp")),
        check_vma=False,
    )
```

```python
import jax
import jax.numpy as jnp
from jax import lax
from jax.experimental import pallas as pl
from jax.experimental.pallas import tpu as pltpu
from jax.sharding import PartitionSpec as P

QUARTERS = 4
HALVES = 2
PIECES = QUARTERS * HALVES
MIB = 1 << 20
LANES = 128
CHIP = 2


def tile_of(width, limit):
    return max(t for t in range(LANES, limit + 1, LANES) if width % t == 0)


def streams_of(width):
    return max(count for count in (1, 2) if width % (count * LANES) == 0)


def in_hbm(x):
    return pltpu.with_memory_space_constraint(x, pltpu.HBM)


def add_rounded(left, right):
    return (left.astype(jnp.float32) + right.astype(jnp.float32)).astype(left.dtype)


class Order:
    def __init__(self):
        self.token = None

    def call(
        self, kernel, operands, out_shape, in_specs=None, out_specs=None, unread=(),
        vmem=6 * MIB, **options,
    ):
        out_shape = list(out_shape)
        whole = pl.BlockSpec(memory_space=pltpu.VMEM)
        anywhere = pl.BlockSpec(memory_space=pl.ANY)
        in_specs = [whole] * len(operands) if in_specs is None else list(in_specs)
        out_specs = [whole] * len(out_shape) if out_specs is None else list(out_specs)
        given, made = len(operands), len(out_shape)
        tokens = [*unread] if self.token is None else [*unread, self.token]

        def body(*refs):
            start = given + len(tokens)
            kernel(*refs[:given], *refs[start:start + made], *refs[start + made + 1:])

        *results, self.token = pl.pallas_call(
            body,
            in_specs=in_specs + [anywhere] * len(tokens),
            out_specs=out_specs + [anywhere],
            out_shape=out_shape + [jax.ShapeDtypeStruct((8, LANES), jnp.float32)],
            compiler_params=pltpu.CompilerParams(vmem_limit_bytes=vmem),
            **options,
        )(*operands, *tokens)
        return results

    def add(self, *pairs, unread=()):
        count = len(pairs)

        def kernel(*refs):
            for i in range(count):
                refs[2 * count + i][...] = add_rounded(refs[2 * i][...], refs[2 * i + 1][...])

        shapes = [jax.ShapeDtypeStruct(x.shape, x.dtype) for x, _ in pairs]
        operands = [x for pair in pairs for x in pair]
        return self.call(kernel, operands, shapes, unread=unread, name="add")


def swap_quarter(x, bits):
    size = lax.axis_size("dp")
    step = bits * (size // QUARTERS)
    return lax.ppermute(x, "dp", [(i, i ^ step) for i in range(size)])


def swap_core(x):
    size = lax.axis_size("mp")
    return lax.ppermute(x, "mp", [(i, i ^ 1) for i in range(size)])


def move_chip(x, pairs):
    return lax.ppermute(
        x, "mp", [(HALVES * a + c, HALVES * b + c) for a, b in pairs for c in range(HALVES)]
    )


class LineSum:
    def __init__(self, place, count):
        self.place, self.count = place, count
        self.chips = lax.axis_size("mp") // HALVES
        self.deepest = self.chips // 2 - 1
        self.lag = 2 * self.deepest + 1
        self.step, self.own, self.sent, self.came = 0, [], [], None

    def swaps(self, odd):
        found = []
        for chip in range(odd, self.chips - 1, 2):
            depths = [min(c, self.chips - 1 - c) for c in (chip, chip + 1)]
            if depths[0] == depths[1]:
                ages = [depths[0]]
            else:
                ages = [min(depths), self.lag - max(depths)]
            if any(0 <= self.step - age < self.count for age in ages):
                found += [(chip, chip + 1), (chip + 1, chip)]
        return found

    def advance(self, order, chunk, unread=()):
        deepest, chips = self.deepest, self.chips
        keep, other = chunk if chunk is not None else (None, None)
        operands = [self.place]
        own = list(self.own)
        if chunk is not None:
            operands += [keep, other]
        base = len(operands)
        history = (own[::-1] + [own[0] if own else keep] * deepest)[:deepest]
        some = keep if keep is not None else own[-1]
        sent = (self.sent[::-1] + [(some, some)] * max(deepest, 1))[:max(deepest, 1)]
        came = self.came if self.came is not None else (some, some)
        operands += history + [x for pair in sent for x in pair] + list(came)
        smem, whole = pl.BlockSpec(memory_space=pltpu.SMEM), pl.BlockSpec(memory_space=pltpu.VMEM)
        fresh = chunk is not None

        def kernel(*refs):
            place_ref, rest = refs[0], refs[base:]
            past = rest[:deepest]
            sents = rest[deepest:deepest + 2 * len(sent)]
            even, odd = rest[deepest + 2 * len(sent):][:2]
            outs = rest[deepest + 2 * len(sent) + 2:]
            even_ref, odd_ref, total_ref = outs[:3]
            if fresh:
                own_ref = outs[3]
                own_ref[...] = add_rounded(refs[1][...], refs[2][...])
            for chip in range(chips):
                depth, left_side = min(chip, chips - 1 - chip), chip < chips // 2
                by_even = left_side == (chip % 2 == 0)
                outer, inner = (odd, even) if by_even else (even, odd)
                to_inner, to_outer = (even_ref, odd_ref) if by_even else (odd_ref, even_ref)
                side = 0 if by_even else 1

                @pl.when(place_ref[CHIP] == chip)
                def _(depth=depth, outer=outer, inner=inner, to_inner=to_inner,
                      to_outer=to_outer, side=side):
                    if depth == 0:
                        to_inner[...] = own_ref[...] if fresh else inner[...]
                    else:
                        to_inner[...] = add_rounded(past[depth - 1][...], outer[...])
                    if depth == deepest:
                        to_outer[...] = add_rounded(sents[side][...], inner[...])
                    else:
                        to_outer[...] = inner[...]
                    if depth == 0:
                        total_ref[...] = to_outer[...]
                    else:
                        total_ref[...] = sents[2 * (depth - 1) + 1 - side][...]

        shape = jax.ShapeDtypeStruct(some.shape, some.dtype)
        even, odd, total, *mine = order.call(
            kernel, operands, [shape] * (4 if fresh else 3),
            [smem] + [whole] * (len(operands) - 1), unread=unread, name="line_step",
        )
        self.own = (own + (mine if fresh else own[-1:]))[-max(deepest, 1):]
        self.sent = (self.sent + [(even, odd)])[-max(deepest, 1):]
        self.came = tuple(
            move_chip(x, swaps) if swaps else x
            for x, swaps in ((even, self.swaps(0)), (odd, self.swaps(1)))
        )
        ready = self.step >= self.lag
        self.step += 1
        return total if ready else None


def join_rows(order, tokens, queries, act_tokens, act_queries):
    length, rank = tokens.shape[0] // HALVES, queries.shape[0] // HALVES
    act_length = act_tokens.shape[0]

    def kernel(
        tokens_ref, queries_ref, act_tokens_ref, act_queries_ref, low_ref, high_ref, act_ref, sems
    ):
        copies = []
        for h, ref in enumerate((low_ref, high_ref)):
            copies += [
                pltpu.make_async_copy(
                    tokens_ref.at[pl.ds(h * length, length)],
                    ref.at[pl.ds(0, length)],
                    sems.at[h, 0],
                ),
                pltpu.make_async_copy(
                    queries_ref.at[pl.ds(h * rank, rank)],
                    ref.at[pl.ds(length, rank)],
                    sems.at[h, 1],
                ),
            ]
        copies.append(
            pltpu.make_async_copy(
                act_tokens_ref, act_ref.at[pl.ds(0, act_length)], sems.at[HALVES, 0]
            )
        )
        for copy in copies:
            copy.start()
        act_ref[act_length:] = act_queries_ref[...]
        for copy in copies:
            copy.wait()

    half = jax.ShapeDtypeStruct((length + rank, tokens.shape[1]), tokens.dtype)
    act = (act_length + act_queries.shape[0], act_tokens.shape[1])
    anywhere, whole = pl.BlockSpec(memory_space=pl.ANY), pl.BlockSpec(memory_space=pltpu.VMEM)
    return order.call(
        kernel,
        [in_hbm(tokens), in_hbm(queries), in_hbm(act_tokens), in_hbm(act_queries)],
        [half, half, jax.ShapeDtypeStruct(act, act_tokens.dtype)],
        [anywhere, anywhere, anywhere, whole],
        scratch_shapes=[pltpu.SemaphoreType.DMA((HALVES + 1, 2))],
        name="join_rows",
    )


def place_rows(place_ref, low_ref, high_ref, rows_ref):
    half = low_ref.shape[0]
    core = place_ref[1]
    rows_ref[pl.ds(pl.multiple_of(core * half, 16), half), :] = low_ref[...]
    rows_ref[pl.ds(pl.multiple_of((1 - core) * half, 16), half), :] = high_ref[...]


def multiply(order, place, low, high, basis, held, unread=()):
    half, depth = low.shape
    width = basis.shape[1]
    first = held is None

    streams = streams_of(width)
    block = width // streams
    tile = tile_of(width, 512)

    def product(rows_ref, basis_ref, keep_refs, send_refs, at):
        terms = jnp.dot(
            rows_ref[...], basis_ref[:, at:at + tile], preferred_element_type=jnp.float32
        ).astype(rows_ref.dtype)
        for b in range(streams):
            start, stop = max(at, b * block), min(at + tile, (b + 1) * block)
            if start < stop:
                columns = slice(start - b * block, stop - b * block)
                keep_refs[b][:, columns] = terms[:half, start - at:stop - at]
                send_refs[b][:, columns] = terms[half:, start - at:stop - at]

    def load_kernel(place_ref, low_ref, high_ref, basis_ref, *refs):
        keep_refs, send_refs = refs[:streams], refs[streams:2 * streams]
        held_ref, rows_ref, sems = refs[2 * streams:]
        copies = [
            pltpu.make_async_copy(
                basis_ref.at[:, pl.ds(at, tile)],
                held_ref.at[:, pl.ds(at, tile)],
                sems.at[at // tile],
            )
            for at in range(0, width, tile)
        ]
        for copy in copies:
            copy.start()
        place_rows(place_ref, low_ref, high_ref, rows_ref)
        for i, copy in enumerate(copies):
            copy.wait()
            product(rows_ref, held_ref, keep_refs, send_refs, i * tile)

    def held_kernel(place_ref, low_ref, high_ref, held_ref, *refs):
        keep_refs, send_refs, rows_ref = refs[:streams], refs[streams:2 * streams], refs[-1]
        place_rows(place_ref, low_ref, high_ref, rows_ref)
        for at in range(0, width, tile):
            product(rows_ref, held_ref, keep_refs, send_refs, at)

    smem = pl.BlockSpec(memory_space=pltpu.SMEM)
    whole = pl.BlockSpec(memory_space=pltpu.VMEM)
    anywhere = pl.BlockSpec(memory_space=pl.ANY)
    outs = [jax.ShapeDtypeStruct((half, block), low.dtype)] * (2 * streams)
    scratch = [pltpu.VMEM((HALVES * half, depth), low.dtype)]
    if first:
        return order.call(
            load_kernel,
            [place, low, high, basis],
            outs + [pltpu.VMEM(basis.shape, basis.dtype)],
            [smem, whole, whole, anywhere],
            scratch_shapes=scratch + [pltpu.SemaphoreType.DMA((width // tile,))],
            name="load_and_multiply",
        )
    held = pltpu.with_memory_space_constraint(held, pltpu.VMEM)
    return order.call(
        held_kernel,
        [place, low, high, held],
        outs,
        [smem, whole, whole, whole],
        unread=unread,
        scratch_shapes=scratch,
        name="multiply",
    )


def multiply_activations(order, rows, basis, unread=()):
    count, depth = rows.shape
    width, half = basis.shape[1], rows.shape[0] // HALVES
    tile = tile_of(width, 256)

    def kernel(rows_ref, basis_ref, low_ref, high_ref):
        for h, ref in enumerate((low_ref, high_ref)):
            terms = jnp.dot(
                rows_ref[h * half:(h + 1) * half, :],
                basis_ref[...],
                preferred_element_type=jnp.float32,
            )
            ref[...] = terms.astype(ref.dtype)

    out = pl.BlockSpec((half, tile), lambda i: (0, i))
    return order.call(
        kernel,
        [in_hbm(rows), in_hbm(basis)],
        [jax.ShapeDtypeStruct((half, width), rows.dtype)] * HALVES,
        [
            pl.BlockSpec((count, depth), lambda i: (0, 0)),
            pl.BlockSpec((depth, tile), lambda i: (0, i)),
        ],
        [out, out],
        unread=unread,
        grid=(width // tile,),
        name="multiply_activations",
    )


def rotated_places(core):
    return [(0, core), (2 - core, core), (1 + core, core), (3, core)]


def correct_kernel(tokens, place_ref, damping_ref, *refs):
    groups = 2 * QUARTERS
    rot_refs, act_refs = refs[:groups], refs[groups:groups + HALVES]
    eig_ref, pre_ref, rot_tok, rot_qry, act_tok, act_qry = refs[groups + HALVES:]
    queries = rot_refs[0].shape[0] - tokens
    quarter, core = place_ref[0], place_ref[1]

    def put(piece, values):
        rot_tok[pl.ds(pl.multiple_of(piece * tokens, 16), tokens), :] = values[:tokens]
        rot_qry[pl.ds(pl.multiple_of(piece * queries, 16), queries), :] = values[tokens:]

    @pl.when(pl.program_id(0) == 0)
    def _():
        per_ref = PIECES // HALVES
        size = tokens + queries
        act_qry[...] = jnp.zeros_like(act_qry)
        for piece in range(PIECES):
            ref, at = act_refs[piece // per_ref], piece % per_ref * size
            row = piece * tokens
            act_tok[row:row + tokens, :] = ref[at:at + tokens, :]
            row = piece * queries
            act_qry[piece // HALVES, row:row + queries, :] = ref[at + tokens:at + size, :]

    for held, refs_held in ((core, rot_refs[:QUARTERS]), (1 - core, rot_refs[QUARTERS:])):
        for (bits, half), ref in zip(rotated_places(held), refs_held):
            put((quarter ^ bits) * HALVES + half, ref[...])

    length = tokens * PIECES // 2
    outs, ins = eig_ref.shape
    token_rows, query_rows = rot_tok[...].T, rot_qry[...].T
    down, across = tile_of(outs, 128), tile_of(ins, 256)
    for at in range(0, outs, down):
        for by in range(0, ins, across):
            rows, columns = slice(at, at + down), slice(by, by + across)
            total = None
            for seq in range(2):
                span = slice(seq * length, (seq + 1) * length)
                rotated = jnp.dot(
                    token_rows[rows, span],
                    act_tok[span, columns],
                    preferred_element_type=jnp.float32,
                )
                square = rotated * rotated
                total = square if total is None else total + square
            eig = total * (1.0 / (2 * length))
            eig_ref[rows, columns] = eig
            inverse = 1.0 / (eig + damping_ref[0])
            for query in range(QUARTERS):
                product = jnp.dot(
                    query_rows[rows],
                    act_qry[query, :, columns],
                    preferred_element_type=jnp.float32,
                )
                pre_ref[query, rows, columns] = (product * inverse).astype(pre_ref.dtype)


def correct(order, tokens, place, damping, rot, act, block, outs, made):
    size, width = rot[0].shape
    rows, ins = act[0].shape
    queries = size - tokens
    tile = tile_of(width, 256)
    steps = width // tile
    smem = pl.BlockSpec(memory_space=pltpu.SMEM)
    dtype = rot[0].dtype
    operands = [place, damping, *rot, *act]
    count, kept = len(operands), len(made)
    return order.call(
        lambda *refs: correct_kernel(tokens, *refs[:count], *refs[count + kept:]),
        operands + list(made),
        [
            jax.ShapeDtypeStruct((outs, ins), jnp.float32),
            jax.ShapeDtypeStruct((QUARTERS, outs, ins), dtype),
        ],
        [smem, smem]
        + [pl.BlockSpec((size, tile), lambda i: (0, i))] * len(rot)
        + [pl.BlockSpec((rows, ins), lambda i: (0, 0))] * len(act)
        + [pl.BlockSpec(memory_space=pl.ANY)] * kept,
        [
            pl.BlockSpec((tile, ins), lambda i: (block * steps + i, 0)),
            pl.BlockSpec((QUARTERS, tile, ins), lambda i: (0, block * steps + i, 0)),
        ],
        input_output_aliases={count + i: i for i in range(kept)},
        grid=(steps,),
        scratch_shapes=[
            pltpu.VMEM((PIECES * tokens, tile), dtype),
            pltpu.VMEM((PIECES * queries, tile), dtype),
            pltpu.VMEM((PIECES * tokens, ins), dtype),
            pltpu.VMEM((QUARTERS, PIECES * queries, ins), dtype),
        ],
        vmem=32 * MIB,
        name="correct",
    )


def outer_rows(tokens, queries):
    size = lax.axis_size("dp")
    index = lax.axis_index("dp")
    step = 1
    while step < size // QUARTERS:
        pairs = [(i, i ^ step) for i in range(size)]
        first = (index // step) % 2 == 0

        def joined(x):
            other = lax.ppermute(x, "dp", pairs)
            return jnp.where(
                first, jnp.concatenate([x, other]), jnp.concatenate([other, x])
            )

        tokens, queries = joined(tokens), joined(queries)
        step *= 2
    return tokens, queries


class QuarterSum:
    def __init__(self, low, high):
        size = lax.axis_size("dp")
        outer = size // QUARTERS
        self.hops = [(outer, 2 * outer), (2 * outer, outer)]
        step = 1
        while step < outer:
            self.hops.append((step, step))
            step *= 2
        self.size, self.pair, self.hop = size, (low, high), 0
        self.send()

    def send(self):
        self.came = [
            lax.ppermute(x, "dp", [(i, i ^ step) for i in range(self.size)])
            for x, step in zip(self.pair, self.hops[self.hop])
        ]

    def add(self, order):
        self.pair = order.add(*zip(self.pair, self.came))
        self.hop += 1
        if self.hop < len(self.hops):
            self.send()


def activation_rows(rows, tokens):
    blocks = lax.all_gather(rows, "mp", axis=0)
    holders, _, width = blocks.shape
    if holders != PIECES:
        blocks = jnp.concatenate(
            [
                blocks[:, :tokens].reshape(PIECES, -1, width),
                blocks[:, tokens:].reshape(PIECES, -1, width),
            ],
            axis=1,
        )
    return blocks.reshape(-1, width)


def shards(out_grads, inputs, out_basis, in_basis, query_out, query_in, damping):
    order = Order()
    dp, mp = lax.axis_index("dp"), lax.axis_index("mp")
    place = jnp.stack(
        [dp // (lax.axis_size("dp") // QUARTERS), mp % HALVES, mp // HALVES]
    ).astype(jnp.int32)

    tokens, queries = outer_rows(out_grads, query_out)
    length = tokens.shape[0] // HALVES
    low, high, act_rows = join_rows(order, tokens, queries, inputs, query_in)
    beside = [swap_quarter(low, 2), swap_quarter(high, 1)]
    behind = [swap_quarter(low, 1), swap_quarter(high, 2)]
    across = [swap_quarter(beside[0], 1), swap_quarter(beside[1], 2)]
    act_rows = activation_rows(act_rows, inputs.shape[0])

    width = out_basis.shape[1]
    lines = [LineSum(place, QUARTERS) for _ in range(streams_of(width))]
    held, acts = None, None
    chunks, late = [], []
    totals, swapped = [[] for _ in lines], [[] for _ in lines]

    def rotate(pair, unread=()):
        nonlocal held
        results = multiply(order, place, *pair, out_basis, held, unread)
        held = results.pop() if held is None else held
        came = [swap_core(x) for x in results[len(lines):]]
        chunks.append(list(zip(results, came)))

    def advance(s, unread=()):
        if s >= len(lines):
            return
        line, pins = lines[s], [*unread, *late]
        late.clear()
        chunk = chunks[line.step][s] if line.step < QUARTERS else None
        total = line.advance(order, chunk, pins)
        if total is not None:
            totals[s].append(total)
            swapped[s].append(swap_core(total))
            late.append(swapped[s][-1])

    def activate(unread=()):
        nonlocal acts
        acts = QuarterSum(*multiply_activations(order, act_rows, in_basis, unread))

    rotate((low, high))
    advance(0)
    advance(1)
    rotate(beside)
    advance(0)
    rotate(behind, [*behind])
    advance(1)
    rotate(across, [*across])
    advance(0)
    advance(1)
    advance(0)
    advance(1)
    activate()
    advance(0)
    advance(1)
    acts.add(order)
    advance(0)
    advance(1)
    acts.add(order)
    advance(0)
    advance(1)
    while acts.hop < len(acts.hops):
        acts.add(order)
    while len(totals[-1]) < QUARTERS:
        for s in range(len(lines)):
            advance(s)

    made = ()
    for s in range(len(lines)):
        rot = totals[s] + swapped[s]
        made = correct(order, length, place, damping, rot, acts.pair, s, width, made)
    return tuple(made)


def solution(mesh):
    placed = (
        P("dp", "mp"),
        P("mp", "dp"),
        P("mp", "dp"),
        P("dp", "mp"),
        P("dp", "mp"),
        P("mp", "dp"),
        P(),
    )
    return jax.shard_map(
        shards,
        mesh=mesh,
        in_specs=placed,
        out_specs=(P("dp", "mp"), P(None, "dp", "mp")),
        check_vma=False,
    )
```

```python
import jax
import jax.numpy as jnp
from jax import lax
from jax.experimental import pallas as pl
from jax.experimental.pallas import tpu as pltpu
from jax.sharding import PartitionSpec as P

QUARTERS = 4
HALVES = 2
PIECES = QUARTERS * HALVES
MIB = 1 << 20
LANES = 128
CHIP = 2


def tile_of(width, limit):
    return max(t for t in range(LANES, limit + 1, LANES) if width % t == 0)


def contract_rows(left, right):
    return lax.dot_general(
        left, right, (((0,), (0,)), ((), ())), preferred_element_type=jnp.float32
    )


def streams_of(width):
    return max(count for count in (1, 2) if width % (count * LANES) == 0)


def in_hbm(x):
    return pltpu.with_memory_space_constraint(x, pltpu.HBM)


def add_rounded(left, right):
    return (left.astype(jnp.float32) + right.astype(jnp.float32)).astype(left.dtype)


class Order:
    def __init__(self):
        self.token = None

    def call(
        self, kernel, operands, out_shape, in_specs=None, out_specs=None, unread=(),
        vmem=6 * MIB, **options,
    ):
        out_shape = list(out_shape)
        whole = pl.BlockSpec(memory_space=pltpu.VMEM)
        anywhere = pl.BlockSpec(memory_space=pl.ANY)
        in_specs = [whole] * len(operands) if in_specs is None else list(in_specs)
        out_specs = [whole] * len(out_shape) if out_specs is None else list(out_specs)
        given, made = len(operands), len(out_shape)
        tokens = [*unread] if self.token is None else [*unread, self.token]

        def body(*refs):
            start = given + len(tokens)
            kernel(*refs[:given], *refs[start:start + made], *refs[start + made + 1:])

        *results, self.token = pl.pallas_call(
            body,
            in_specs=in_specs + [anywhere] * len(tokens),
            out_specs=out_specs + [anywhere],
            out_shape=out_shape + [jax.ShapeDtypeStruct((8, LANES), jnp.float32)],
            compiler_params=pltpu.CompilerParams(vmem_limit_bytes=vmem),
            **options,
        )(*operands, *tokens)
        return results

    def add(self, *pairs, unread=()):
        count = len(pairs)

        def kernel(*refs):
            for i in range(count):
                refs[2 * count + i][...] = add_rounded(refs[2 * i][...], refs[2 * i + 1][...])

        shapes = [jax.ShapeDtypeStruct(x.shape, x.dtype) for x, _ in pairs]
        operands = [x for pair in pairs for x in pair]
        return self.call(kernel, operands, shapes, unread=unread, name="add")


def swap_quarter(x, bits):
    size = lax.axis_size("dp")
    step = bits * (size // QUARTERS)
    return lax.ppermute(x, "dp", [(i, i ^ step) for i in range(size)])


def swap_core(x):
    size = lax.axis_size("mp")
    return lax.ppermute(x, "mp", [(i, i ^ 1) for i in range(size)])


def move_chip(x, pairs):
    return lax.ppermute(
        x, "mp", [(HALVES * a + c, HALVES * b + c) for a, b in pairs for c in range(HALVES)]
    )


class LineSum:
    def __init__(self, place, count):
        self.place, self.count = place, count
        self.chips = lax.axis_size("mp") // HALVES
        self.deepest = self.chips // 2 - 1
        self.lag = 2 * self.deepest + 1
        self.step, self.own, self.sent, self.came = 0, [], [], None

    def swaps(self, odd):
        found = []
        for chip in range(odd, self.chips - 1, 2):
            depths = [min(c, self.chips - 1 - c) for c in (chip, chip + 1)]
            if depths[0] == depths[1]:
                ages = [depths[0]]
            else:
                ages = [min(depths), self.lag - max(depths)]
            if any(0 <= self.step - age < self.count for age in ages):
                found += [(chip, chip + 1), (chip + 1, chip)]
        return found

    def advance(self, order, chunk, unread=()):
        deepest, chips = self.deepest, self.chips
        keep, other = chunk if chunk is not None else (None, None)
        operands = [self.place]
        own = list(self.own)
        if chunk is not None:
            operands += [keep, other]
        base = len(operands)
        history = (own[::-1] + [own[0] if own else keep] * deepest)[:deepest]
        some = keep if keep is not None else own[-1]
        sent = (self.sent[::-1] + [(some, some)] * max(deepest, 1))[:max(deepest, 1)]
        came = self.came if self.came is not None else (some, some)
        operands += history + [x for pair in sent for x in pair] + list(came)
        smem, whole = pl.BlockSpec(memory_space=pltpu.SMEM), pl.BlockSpec(memory_space=pltpu.VMEM)
        fresh = chunk is not None

        def kernel(*refs):
            place_ref, rest = refs[0], refs[base:]
            past = rest[:deepest]
            sents = rest[deepest:deepest + 2 * len(sent)]
            even, odd = rest[deepest + 2 * len(sent):][:2]
            outs = rest[deepest + 2 * len(sent) + 2:]
            even_ref, odd_ref, total_ref = outs[:3]
            if fresh:
                own_ref = outs[3]
                own_ref[...] = add_rounded(refs[1][...], refs[2][...])
            for chip in range(chips):
                depth, left_side = min(chip, chips - 1 - chip), chip < chips // 2
                by_even = left_side == (chip % 2 == 0)
                outer, inner = (odd, even) if by_even else (even, odd)
                to_inner, to_outer = (even_ref, odd_ref) if by_even else (odd_ref, even_ref)
                side = 0 if by_even else 1

                @pl.when(place_ref[CHIP] == chip)
                def _(depth=depth, outer=outer, inner=inner, to_inner=to_inner,
                      to_outer=to_outer, side=side):
                    if depth == 0:
                        to_inner[...] = own_ref[...] if fresh else inner[...]
                    else:
                        to_inner[...] = add_rounded(past[depth - 1][...], outer[...])
                    if depth == deepest:
                        to_outer[...] = add_rounded(sents[side][...], inner[...])
                    else:
                        to_outer[...] = inner[...]
                    if depth == 0:
                        total_ref[...] = to_outer[...]
                    else:
                        total_ref[...] = sents[2 * (depth - 1) + 1 - side][...]

        shape = jax.ShapeDtypeStruct(some.shape, some.dtype)
        even, odd, total, *mine = order.call(
            kernel, operands, [shape] * (4 if fresh else 3),
            [smem] + [whole] * (len(operands) - 1), unread=unread, name="line_step",
        )
        self.own = (own + (mine if fresh else own[-1:]))[-max(deepest, 1):]
        self.sent = (self.sent + [(even, odd)])[-max(deepest, 1):]
        self.came = tuple(
            move_chip(x, swaps) if swaps else x
            for x, swaps in ((even, self.swaps(0)), (odd, self.swaps(1)))
        )
        ready = self.step >= self.lag
        self.step += 1
        return total if ready else None


def join_rows(order, tokens, queries):
    length, rank = tokens.shape[0] // HALVES, queries.shape[0] // HALVES

    def kernel(tokens_ref, queries_ref, low_ref, high_ref, sems):
        copies = []
        for h, ref in enumerate((low_ref, high_ref)):
            copies += [
                pltpu.make_async_copy(
                    tokens_ref.at[pl.ds(h * length, length)],
                    ref.at[pl.ds(0, length)],
                    sems.at[h, 0],
                ),
                pltpu.make_async_copy(
                    queries_ref.at[pl.ds(h * rank, rank)],
                    ref.at[pl.ds(length, rank)],
                    sems.at[h, 1],
                ),
            ]
        for copy in copies:
            copy.start()
        for copy in copies:
            copy.wait()

    half = jax.ShapeDtypeStruct((length + rank, tokens.shape[1]), tokens.dtype)
    anywhere = pl.BlockSpec(memory_space=pl.ANY)
    return order.call(
        kernel,
        [in_hbm(tokens), in_hbm(queries)],
        [half, half],
        [anywhere, anywhere],
        scratch_shapes=[pltpu.SemaphoreType.DMA((HALVES, 2))],
        name="join_rows",
    )


def place_rows(place_ref, low_ref, high_ref, rows_ref):
    half = low_ref.shape[0]
    core = place_ref[1]
    rows_ref[pl.ds(pl.multiple_of(core * half, 16), half), :] = low_ref[...]
    rows_ref[pl.ds(pl.multiple_of((1 - core) * half, 16), half), :] = high_ref[...]


def multiply(order, place, low, high, basis, held, unread=()):
    half, depth = low.shape
    width = basis.shape[1]
    first = held is None

    streams = streams_of(width)
    block = width // streams
    tile = tile_of(width, 512)

    def product(rows_ref, basis_ref, keep_refs, send_refs, at):
        terms = jnp.dot(
            rows_ref[...], basis_ref[:, at:at + tile], preferred_element_type=jnp.float32
        ).astype(rows_ref.dtype)
        for b in range(streams):
            start, stop = max(at, b * block), min(at + tile, (b + 1) * block)
            if start < stop:
                columns = slice(start - b * block, stop - b * block)
                keep_refs[b][:, columns] = terms[:half, start - at:stop - at]
                send_refs[b][:, columns] = terms[half:, start - at:stop - at]

    def load_kernel(place_ref, low_ref, high_ref, basis_ref, *refs):
        keep_refs, send_refs = refs[:streams], refs[streams:2 * streams]
        held_ref, rows_ref, sems = refs[2 * streams:]
        copies = [
            pltpu.make_async_copy(
                basis_ref.at[:, pl.ds(at, tile)],
                held_ref.at[:, pl.ds(at, tile)],
                sems.at[at // tile],
            )
            for at in range(0, width, tile)
        ]
        for copy in copies:
            copy.start()
        place_rows(place_ref, low_ref, high_ref, rows_ref)
        for i, copy in enumerate(copies):
            copy.wait()
            product(rows_ref, held_ref, keep_refs, send_refs, i * tile)

    def held_kernel(place_ref, low_ref, high_ref, held_ref, *refs):
        keep_refs, send_refs, rows_ref = refs[:streams], refs[streams:2 * streams], refs[-1]
        place_rows(place_ref, low_ref, high_ref, rows_ref)
        for at in range(0, width, tile):
            product(rows_ref, held_ref, keep_refs, send_refs, at)

    smem = pl.BlockSpec(memory_space=pltpu.SMEM)
    whole = pl.BlockSpec(memory_space=pltpu.VMEM)
    anywhere = pl.BlockSpec(memory_space=pl.ANY)
    outs = [jax.ShapeDtypeStruct((half, block), low.dtype)] * (2 * streams)
    scratch = [pltpu.VMEM((HALVES * half, depth), low.dtype)]
    if first:
        return order.call(
            load_kernel,
            [place, low, high, basis],
            outs + [pltpu.VMEM(basis.shape, basis.dtype)],
            [smem, whole, whole, anywhere],
            scratch_shapes=scratch + [pltpu.SemaphoreType.DMA((width // tile,))],
            name="load_and_multiply",
        )
    held = pltpu.with_memory_space_constraint(held, pltpu.VMEM)
    return order.call(
        held_kernel,
        [place, low, high, held],
        outs,
        [smem, whole, whole, whole],
        unread=unread,
        scratch_shapes=scratch,
        name="multiply",
    )


def multiply_activations(order, tokens, queries, basis, unread=()):
    depth, width = basis.shape
    length, rank = tokens.shape[0] // PIECES, queries.shape[0] // PIECES
    per_half, size = PIECES // HALVES, length + rank
    tile = tile_of(width, 256)

    def kernel(tokens_ref, queries_ref, basis_ref, *half_refs):
        for rows_ref, count, at in ((tokens_ref, length, 0), (queries_ref, rank, length)):
            terms = jnp.dot(
                rows_ref[...], basis_ref[...], preferred_element_type=jnp.float32
            ).astype(rows_ref.dtype)
            for piece in range(PIECES):
                start = piece % per_half * size + at
                ref = half_refs[piece // per_half]
                ref[start:start + count, :] = terms[piece * count:(piece + 1) * count]

    out = pl.BlockSpec((per_half * size, tile), lambda i: (0, i))
    return order.call(
        kernel,
        [in_hbm(tokens), queries, in_hbm(basis)],
        [jax.ShapeDtypeStruct((per_half * size, width), tokens.dtype)] * HALVES,
        [
            pl.BlockSpec(tokens.shape, lambda i: (0, 0)),
            pl.BlockSpec(queries.shape, lambda i: (0, 0)),
            pl.BlockSpec((depth, tile), lambda i: (0, i)),
        ],
        [out, out],
        unread=unread,
        grid=(width // tile,),
        vmem=16 * MIB,
        name="multiply_activations",
    )


def rotated_places(core):
    return [(0, core), (2 - core, core), (1 + core, core), (3, core)]


def correct_kernel(tokens, place_ref, damping_ref, *refs):
    groups = 2 * QUARTERS
    rot_refs, act_refs = refs[:groups], refs[groups:groups + HALVES]
    eig_ref, pre_ref, rot_tok, rot_qry, act_tok, act_qry = refs[groups + HALVES:]
    queries = rot_refs[0].shape[0] - tokens
    quarter, core = place_ref[0], place_ref[1]

    def put(tok, qry, piece, values):
        tok[pl.ds(pl.multiple_of(piece * tokens, 16), tokens), :] = values[:tokens]
        qry[pl.ds(pl.multiple_of(piece * queries, 16), queries), :] = values[tokens:]

    @pl.when(pl.program_id(0) == 0)
    def _():
        per_ref = PIECES // HALVES
        size = tokens + queries
        for piece in range(PIECES):
            at = piece % per_ref * size
            put(act_tok, act_qry, piece, act_refs[piece // per_ref][at:at + size, :])

    for held, refs_held in ((core, rot_refs[:QUARTERS]), (1 - core, rot_refs[QUARTERS:])):
        for (bits, half), ref in zip(rotated_places(held), refs_held):
            put(rot_tok, rot_qry, (quarter ^ bits) * HALVES + half, ref[...])

    length = tokens * PIECES // 2
    total = None
    for seq in range(2):
        rows = slice(seq * length, (seq + 1) * length)
        rotated = contract_rows(rot_tok[rows, :], act_tok[rows, :])
        square = rotated * rotated
        total = square if total is None else total + square
    eig = total * (1.0 / (2 * length))
    eig_ref[...] = eig
    inverse = 1.0 / (eig + damping_ref[0])
    rank = queries * HALVES
    for query in range(QUARTERS):
        rows = slice(query * rank, (query + 1) * rank)
        product = contract_rows(rot_qry[rows, :], act_qry[rows, :])
        pre_ref[query] = (product * inverse).astype(pre_ref.dtype)


def correct(order, tokens, place, damping, rot, act, block, outs, made):
    size, width = rot[0].shape
    rows, ins = act[0].shape
    queries = size - tokens
    tile = tile_of(width, 256)
    steps = width // tile
    smem = pl.BlockSpec(memory_space=pltpu.SMEM)
    dtype = rot[0].dtype
    operands = [place, damping, *rot, *act]
    count, kept = len(operands), len(made)
    return order.call(
        lambda *refs: correct_kernel(tokens, *refs[:count], *refs[count + kept:]),
        operands + list(made),
        [
            jax.ShapeDtypeStruct((outs, ins), jnp.float32),
            jax.ShapeDtypeStruct((QUARTERS, outs, ins), dtype),
        ],
        [smem, smem]
        + [pl.BlockSpec((size, tile), lambda i: (0, i))] * len(rot)
        + [pl.BlockSpec((rows, ins), lambda i: (0, 0))] * len(act)
        + [pl.BlockSpec(memory_space=pl.ANY)] * kept,
        [
            pl.BlockSpec((tile, ins), lambda i: (block * steps + i, 0)),
            pl.BlockSpec((QUARTERS, tile, ins), lambda i: (0, block * steps + i, 0)),
        ],
        input_output_aliases={count + i: i for i in range(kept)},
        grid=(steps,),
        scratch_shapes=[
            pltpu.VMEM((PIECES * tokens, tile), dtype),
            pltpu.VMEM((PIECES * queries, tile), dtype),
            pltpu.VMEM((PIECES * tokens, ins), dtype),
            pltpu.VMEM((PIECES * queries, ins), dtype),
        ],
        vmem=32 * MIB,
        name="correct",
    )


def outer_rows(tokens, queries):
    size = lax.axis_size("dp")
    index = lax.axis_index("dp")
    step = 1
    while step < size // QUARTERS:
        pairs = [(i, i ^ step) for i in range(size)]
        first = (index // step) % 2 == 0

        def joined(x):
            other = lax.ppermute(x, "dp", pairs)
            return jnp.where(
                first, jnp.concatenate([x, other]), jnp.concatenate([other, x])
            )

        tokens, queries = joined(tokens), joined(queries)
        step *= 2
    return tokens, queries


class QuarterSum:
    def __init__(self, low, high):
        size = lax.axis_size("dp")
        outer = size // QUARTERS
        self.hops = [(outer, 2 * outer), (2 * outer, outer)]
        step = 1
        while step < outer:
            self.hops.append((step, step))
            step *= 2
        self.size, self.pair, self.hop = size, (low, high), 0
        self.send()

    def send(self):
        self.came = [
            lax.ppermute(x, "dp", [(i, i ^ step) for i in range(self.size)])
            for x, step in zip(self.pair, self.hops[self.hop])
        ]

    def add(self, order):
        self.pair = order.add(*zip(self.pair, self.came))
        self.hop += 1
        if self.hop < len(self.hops):
            self.send()


def doubled(x):
    size, index = lax.axis_size("mp"), lax.axis_index("mp")
    step = 1
    while step < size:
        other = lax.ppermute(x, "mp", [(i, i ^ step) for i in range(size)])
        first = (index // step) % 2 == 0
        x = jnp.where(first, jnp.concatenate([x, other]), jnp.concatenate([other, x]))
        step *= 2
    return x


def shards(out_grads, inputs, out_basis, in_basis, query_out, query_in, damping):
    order = Order()
    dp, mp = lax.axis_index("dp"), lax.axis_index("mp")
    place = jnp.stack(
        [dp // (lax.axis_size("dp") // QUARTERS), mp % HALVES, mp // HALVES]
    ).astype(jnp.int32)

    tokens, queries = outer_rows(out_grads, query_out)
    length = tokens.shape[0] // HALVES
    low, high = join_rows(order, tokens, queries)
    beside = [swap_quarter(low, 2), swap_quarter(high, 1)]
    behind = [swap_quarter(low, 1), swap_quarter(high, 2)]
    across = [swap_quarter(beside[0], 1), swap_quarter(beside[1], 2)]
    act_rows = lax.all_gather(inputs, "mp", axis=0, tiled=True)
    act_queries = doubled(query_in)

    width = out_basis.shape[1]
    lines = [LineSum(place, QUARTERS) for _ in range(streams_of(width))]
    held, acts = None, None
    chunks, late = [], []
    totals, swapped = [[] for _ in lines], [[] for _ in lines]

    def rotate(pair, unread=()):
        nonlocal held
        results = multiply(order, place, *pair, out_basis, held, unread)
        held = results.pop() if held is None else held
        came = [swap_core(x) for x in results[len(lines):]]
        chunks.append(list(zip(results, came)))

    def advance(s, unread=()):
        if s >= len(lines):
            return
        line, pins = lines[s], [*unread, *late]
        late.clear()
        chunk = chunks[line.step][s] if line.step < QUARTERS else None
        total = line.advance(order, chunk, pins)
        if total is not None:
            totals[s].append(total)
            swapped[s].append(swap_core(total))
            late.append(swapped[s][-1])

    def activate(unread=()):
        nonlocal acts
        acts = QuarterSum(*multiply_activations(order, act_rows, act_queries, in_basis, unread))

    rotate((low, high))
    advance(0)
    advance(1)
    rotate(beside)
    advance(0)
    rotate(behind, [*behind])
    advance(1)
    rotate(across, [*across])
    advance(0, [act_rows])
    advance(1)
    advance(0)
    advance(1)
    activate()
    advance(0)
    advance(1)
    acts.add(order)
    advance(0)
    advance(1)
    acts.add(order)
    advance(0)
    advance(1)
    while acts.hop < len(acts.hops):
        acts.add(order)
    while len(totals[-1]) < QUARTERS:
        for s in range(len(lines)):
            advance(s)

    made = ()
    for s in range(len(lines)):
        rot = totals[s] + swapped[s]
        made = correct(order, length, place, damping, rot, acts.pair, s, width, made)
    return tuple(made)


def solution(mesh):
    placed = (
        P("dp", "mp"),
        P("mp", "dp"),
        P("mp", "dp"),
        P("dp", "mp"),
        P("dp", "mp"),
        P("mp", "dp"),
        P(),
    )
    return jax.shard_map(
        shards,
        mesh=mesh,
        in_specs=placed,
        out_specs=(P("dp", "mp"), P(None, "dp", "mp")),
        check_vma=False,
    )
```

```python
import jax
import jax.numpy as jnp
from jax import lax
from jax.experimental import pallas as pl
from jax.experimental.pallas import tpu as pltpu
from jax.sharding import PartitionSpec as P

QUARTERS = 4
HALVES = 2
PIECES = QUARTERS * HALVES
MIB = 1 << 20
LANES = 128
CHIP = 2


def tile_of(width, limit):
    return max(t for t in range(LANES, limit + 1, LANES) if width % t == 0)


def contract_rows(left, right):
    return lax.dot_general(
        left, right, (((0,), (0,)), ((), ())), preferred_element_type=jnp.float32
    )


def streams_of(width):
    return max(count for count in (1, 2) if width % (count * LANES) == 0)


def in_hbm(x):
    return pltpu.with_memory_space_constraint(x, pltpu.HBM)


def add_rounded(left, right):
    return (left.astype(jnp.float32) + right.astype(jnp.float32)).astype(left.dtype)


class Order:
    def __init__(self):
        self.token = None

    def call(
        self, kernel, operands, out_shape, in_specs=None, out_specs=None, unread=(),
        vmem=6 * MIB, **options,
    ):
        out_shape = list(out_shape)
        whole = pl.BlockSpec(memory_space=pltpu.VMEM)
        anywhere = pl.BlockSpec(memory_space=pl.ANY)
        in_specs = [whole] * len(operands) if in_specs is None else list(in_specs)
        out_specs = [whole] * len(out_shape) if out_specs is None else list(out_specs)
        given, made = len(operands), len(out_shape)
        tokens = [*unread] if self.token is None else [*unread, self.token]

        def body(*refs):
            start = given + len(tokens)
            kernel(*refs[:given], *refs[start:start + made], *refs[start + made + 1:])

        *results, self.token = pl.pallas_call(
            body,
            in_specs=in_specs + [anywhere] * len(tokens),
            out_specs=out_specs + [anywhere],
            out_shape=out_shape + [jax.ShapeDtypeStruct((8, LANES), jnp.float32)],
            compiler_params=pltpu.CompilerParams(vmem_limit_bytes=vmem),
            **options,
        )(*operands, *tokens)
        return results

    def add(self, *pairs, unread=()):
        count = len(pairs)

        def kernel(*refs):
            for i in range(count):
                refs[2 * count + i][...] = add_rounded(refs[2 * i][...], refs[2 * i + 1][...])

        shapes = [jax.ShapeDtypeStruct(x.shape, x.dtype) for x, _ in pairs]
        operands = [x for pair in pairs for x in pair]
        return self.call(kernel, operands, shapes, unread=unread, name="add")


def swap_quarter(x, bits):
    size = lax.axis_size("dp")
    step = bits * (size // QUARTERS)
    return lax.ppermute(x, "dp", [(i, i ^ step) for i in range(size)])


def swap_core(x):
    size = lax.axis_size("mp")
    return lax.ppermute(x, "mp", [(i, i ^ 1) for i in range(size)])


def move_chip(x, pairs):
    return lax.ppermute(
        x, "mp", [(HALVES * a + c, HALVES * b + c) for a, b in pairs for c in range(HALVES)]
    )


class LineSum:
    def __init__(self, place, count):
        self.place, self.count = place, count
        self.chips = lax.axis_size("mp") // HALVES
        self.deepest = self.chips // 2 - 1
        self.lag = 2 * self.deepest + 1
        self.step, self.own, self.sent, self.came = 0, [], [], None

    def swaps(self, odd):
        found = []
        for chip in range(odd, self.chips - 1, 2):
            depths = [min(c, self.chips - 1 - c) for c in (chip, chip + 1)]
            if depths[0] == depths[1]:
                ages = [depths[0]]
            else:
                ages = [min(depths), self.lag - max(depths)]
            if any(0 <= self.step - age < self.count for age in ages):
                found += [(chip, chip + 1), (chip + 1, chip)]
        return found

    def advance(self, order, chunk, unread=()):
        deepest, chips = self.deepest, self.chips
        keep, other = chunk if chunk is not None else (None, None)
        operands = [self.place]
        own = list(self.own)
        if chunk is not None:
            operands += [keep, other]
        base = len(operands)
        history = (own[::-1] + [own[0] if own else keep] * deepest)[:deepest]
        some = keep if keep is not None else own[-1]
        sent = (self.sent[::-1] + [(some, some)] * max(deepest, 1))[:max(deepest, 1)]
        came = self.came if self.came is not None else (some, some)
        operands += history + [x for pair in sent for x in pair] + list(came)
        smem, whole = pl.BlockSpec(memory_space=pltpu.SMEM), pl.BlockSpec(memory_space=pltpu.VMEM)
        fresh = chunk is not None

        def kernel(*refs):
            place_ref, rest = refs[0], refs[base:]
            past = rest[:deepest]
            sents = rest[deepest:deepest + 2 * len(sent)]
            even, odd = rest[deepest + 2 * len(sent):][:2]
            outs = rest[deepest + 2 * len(sent) + 2:]
            even_ref, odd_ref, total_ref = outs[:3]
            if fresh:
                own_ref = outs[3]
                own_ref[...] = add_rounded(refs[1][...], refs[2][...])
            for chip in range(chips):
                depth, left_side = min(chip, chips - 1 - chip), chip < chips // 2
                by_even = left_side == (chip % 2 == 0)
                outer, inner = (odd, even) if by_even else (even, odd)
                to_inner, to_outer = (even_ref, odd_ref) if by_even else (odd_ref, even_ref)
                side = 0 if by_even else 1

                @pl.when(place_ref[CHIP] == chip)
                def _(depth=depth, outer=outer, inner=inner, to_inner=to_inner,
                      to_outer=to_outer, side=side):
                    if depth == 0:
                        to_inner[...] = own_ref[...] if fresh else inner[...]
                    else:
                        to_inner[...] = add_rounded(past[depth - 1][...], outer[...])
                    if depth == deepest:
                        to_outer[...] = add_rounded(sents[side][...], inner[...])
                    else:
                        to_outer[...] = inner[...]
                    if depth == 0:
                        total_ref[...] = to_outer[...]
                    else:
                        total_ref[...] = sents[2 * (depth - 1) + 1 - side][...]

        shape = jax.ShapeDtypeStruct(some.shape, some.dtype)
        even, odd, total, *mine = order.call(
            kernel, operands, [shape] * (4 if fresh else 3),
            [smem] + [whole] * (len(operands) - 1), unread=unread, name="line_step",
        )
        self.own = (own + (mine if fresh else own[-1:]))[-max(deepest, 1):]
        self.sent = (self.sent + [(even, odd)])[-max(deepest, 1):]
        self.came = tuple(
            move_chip(x, swaps) if swaps else x
            for x, swaps in ((even, self.swaps(0)), (odd, self.swaps(1)))
        )
        ready = self.step >= self.lag
        self.step += 1
        return total if ready else None


def join_rows(order, tokens, queries, act_tokens, act_queries):
    length, rank = tokens.shape[0] // HALVES, queries.shape[0] // HALVES
    act_length = act_tokens.shape[0]

    def kernel(
        tokens_ref, queries_ref, act_tokens_ref, act_queries_ref, low_ref, high_ref, act_ref, sems
    ):
        copies = []
        for h, ref in enumerate((low_ref, high_ref)):
            copies += [
                pltpu.make_async_copy(
                    tokens_ref.at[pl.ds(h * length, length)],
                    ref.at[pl.ds(0, length)],
                    sems.at[h, 0],
                ),
                pltpu.make_async_copy(
                    queries_ref.at[pl.ds(h * rank, rank)],
                    ref.at[pl.ds(length, rank)],
                    sems.at[h, 1],
                ),
            ]
        copies.append(
            pltpu.make_async_copy(
                act_tokens_ref, act_ref.at[pl.ds(0, act_length)], sems.at[HALVES, 0]
            )
        )
        for copy in copies:
            copy.start()
        act_ref[act_length:] = act_queries_ref[...]
        for copy in copies:
            copy.wait()

    half = jax.ShapeDtypeStruct((length + rank, tokens.shape[1]), tokens.dtype)
    act = (act_length + act_queries.shape[0], act_tokens.shape[1])
    anywhere, whole = pl.BlockSpec(memory_space=pl.ANY), pl.BlockSpec(memory_space=pltpu.VMEM)
    return order.call(
        kernel,
        [in_hbm(tokens), in_hbm(queries), in_hbm(act_tokens), in_hbm(act_queries)],
        [half, half, jax.ShapeDtypeStruct(act, act_tokens.dtype)],
        [anywhere, anywhere, anywhere, whole],
        scratch_shapes=[pltpu.SemaphoreType.DMA((HALVES + 1, 2))],
        name="join_rows",
    )


def place_rows(place_ref, low_ref, high_ref, rows_ref):
    half = low_ref.shape[0]
    core = place_ref[1]
    rows_ref[pl.ds(pl.multiple_of(core * half, 16), half), :] = low_ref[...]
    rows_ref[pl.ds(pl.multiple_of((1 - core) * half, 16), half), :] = high_ref[...]


def multiply(order, place, low, high, basis, held, unread=()):
    half, depth = low.shape
    width = basis.shape[1]
    first = held is None

    streams = streams_of(width)
    block = width // streams
    tile = tile_of(width, 512)

    def product(rows_ref, basis_ref, keep_refs, send_refs, at):
        terms = jnp.dot(
            rows_ref[...], basis_ref[:, at:at + tile], preferred_element_type=jnp.float32
        ).astype(rows_ref.dtype)
        for b in range(streams):
            start, stop = max(at, b * block), min(at + tile, (b + 1) * block)
            if start < stop:
                columns = slice(start - b * block, stop - b * block)
                keep_refs[b][:, columns] = terms[:half, start - at:stop - at]
                send_refs[b][:, columns] = terms[half:, start - at:stop - at]

    def load_kernel(place_ref, low_ref, high_ref, basis_ref, *refs):
        keep_refs, send_refs = refs[:streams], refs[streams:2 * streams]
        held_ref, rows_ref, sems = refs[2 * streams:]
        copies = [
            pltpu.make_async_copy(
                basis_ref.at[:, pl.ds(at, tile)],
                held_ref.at[:, pl.ds(at, tile)],
                sems.at[at // tile],
            )
            for at in range(0, width, tile)
        ]
        for copy in copies:
            copy.start()
        place_rows(place_ref, low_ref, high_ref, rows_ref)
        for i, copy in enumerate(copies):
            copy.wait()
            product(rows_ref, held_ref, keep_refs, send_refs, i * tile)

    def held_kernel(place_ref, low_ref, high_ref, held_ref, *refs):
        keep_refs, send_refs, rows_ref = refs[:streams], refs[streams:2 * streams], refs[-1]
        place_rows(place_ref, low_ref, high_ref, rows_ref)
        for at in range(0, width, tile):
            product(rows_ref, held_ref, keep_refs, send_refs, at)

    smem = pl.BlockSpec(memory_space=pltpu.SMEM)
    whole = pl.BlockSpec(memory_space=pltpu.VMEM)
    anywhere = pl.BlockSpec(memory_space=pl.ANY)
    outs = [jax.ShapeDtypeStruct((half, block), low.dtype)] * (2 * streams)
    scratch = [pltpu.VMEM((HALVES * half, depth), low.dtype)]
    if first:
        return order.call(
            load_kernel,
            [place, low, high, basis],
            outs + [pltpu.VMEM(basis.shape, basis.dtype)],
            [smem, whole, whole, anywhere],
            scratch_shapes=scratch + [pltpu.SemaphoreType.DMA((width // tile,))],
            name="load_and_multiply",
        )
    held = pltpu.with_memory_space_constraint(held, pltpu.VMEM)
    return order.call(
        held_kernel,
        [place, low, high, held],
        outs,
        [smem, whole, whole, whole],
        unread=unread,
        scratch_shapes=scratch,
        name="multiply",
    )


def multiply_activations(order, rows, basis, unread=()):
    count, depth = rows.shape
    width, half = basis.shape[1], rows.shape[0] // HALVES
    tile = tile_of(width, 256)

    def kernel(rows_ref, basis_ref, low_ref, high_ref):
        for h, ref in enumerate((low_ref, high_ref)):
            terms = jnp.dot(
                rows_ref[h * half:(h + 1) * half, :],
                basis_ref[...],
                preferred_element_type=jnp.float32,
            )
            ref[...] = terms.astype(ref.dtype)

    out = pl.BlockSpec((half, tile), lambda i: (0, i))
    return order.call(
        kernel,
        [in_hbm(rows), in_hbm(basis)],
        [jax.ShapeDtypeStruct((half, width), rows.dtype)] * HALVES,
        [
            pl.BlockSpec((count, depth), lambda i: (0, 0)),
            pl.BlockSpec((depth, tile), lambda i: (0, i)),
        ],
        [out, out],
        unread=unread,
        grid=(width // tile,),
        name="multiply_activations",
    )


def rotated_places(core):
    return [(0, core), (2 - core, core), (1 + core, core), (3, core)]


def correct_kernel(tokens, place_ref, damping_ref, *refs):
    groups = 2 * QUARTERS
    rot_refs, act_refs = refs[:groups], refs[groups:groups + HALVES]
    eig_ref, pre_ref, rot_tok, rot_qry, act_tok, act_qry = refs[groups + HALVES:]
    queries = rot_refs[0].shape[0] - tokens
    quarter, core = place_ref[0], place_ref[1]

    def put(tok, qry, piece, values):
        tok[pl.ds(pl.multiple_of(piece * tokens, 16), tokens), :] = values[:tokens]
        qry[pl.ds(pl.multiple_of(piece * queries, 16), queries), :] = values[tokens:]

    @pl.when(pl.program_id(0) == 0)
    def _():
        per_ref = PIECES // HALVES
        size = tokens + queries
        for piece in range(PIECES):
            at = piece % per_ref * size
            put(act_tok, act_qry, piece, act_refs[piece // per_ref][at:at + size, :])

    for held, refs_held in ((core, rot_refs[:QUARTERS]), (1 - core, rot_refs[QUARTERS:])):
        for (bits, half), ref in zip(rotated_places(held), refs_held):
            put(rot_tok, rot_qry, (quarter ^ bits) * HALVES + half, ref[...])

    length = tokens * PIECES // 2
    total = None
    for seq in range(2):
        rows = slice(seq * length, (seq + 1) * length)
        rotated = contract_rows(rot_tok[rows, :], act_tok[rows, :])
        square = rotated * rotated
        total = square if total is None else total + square
    eig = total * (1.0 / (2 * length))
    eig_ref[...] = eig
    inverse = 1.0 / (eig + damping_ref[0])
    rank = queries * HALVES
    for query in range(QUARTERS):
        rows = slice(query * rank, (query + 1) * rank)
        product = contract_rows(rot_qry[rows, :], act_qry[rows, :])
        pre_ref[query] = (product * inverse).astype(pre_ref.dtype)


def correct(order, tokens, place, damping, rot, act, block, outs, made):
    size, width = rot[0].shape
    rows, ins = act[0].shape
    queries = size - tokens
    tile = tile_of(width, 256)
    steps = width // tile
    smem = pl.BlockSpec(memory_space=pltpu.SMEM)
    dtype = rot[0].dtype
    operands = [place, damping, *rot, *act]
    count, kept = len(operands), len(made)
    return order.call(
        lambda *refs: correct_kernel(tokens, *refs[:count], *refs[count + kept:]),
        operands + list(made),
        [
            jax.ShapeDtypeStruct((outs, ins), jnp.float32),
            jax.ShapeDtypeStruct((QUARTERS, outs, ins), dtype),
        ],
        [smem, smem]
        + [pl.BlockSpec((size, tile), lambda i: (0, i))] * len(rot)
        + [pl.BlockSpec((rows, ins), lambda i: (0, 0))] * len(act)
        + [pl.BlockSpec(memory_space=pl.ANY)] * kept,
        [
            pl.BlockSpec((tile, ins), lambda i: (block * steps + i, 0)),
            pl.BlockSpec((QUARTERS, tile, ins), lambda i: (0, block * steps + i, 0)),
        ],
        input_output_aliases={count + i: i for i in range(kept)},
        grid=(steps,),
        scratch_shapes=[
            pltpu.VMEM((PIECES * tokens, tile), dtype),
            pltpu.VMEM((PIECES * queries, tile), dtype),
            pltpu.VMEM((PIECES * tokens, ins), dtype),
            pltpu.VMEM((PIECES * queries, ins), dtype),
        ],
        vmem=32 * MIB,
        name="correct",
    )


def outer_rows(tokens, queries):
    size = lax.axis_size("dp")
    index = lax.axis_index("dp")
    step = 1
    while step < size // QUARTERS:
        pairs = [(i, i ^ step) for i in range(size)]
        first = (index // step) % 2 == 0

        def joined(x):
            other = lax.ppermute(x, "dp", pairs)
            return jnp.where(
                first, jnp.concatenate([x, other]), jnp.concatenate([other, x])
            )

        tokens, queries = joined(tokens), joined(queries)
        step *= 2
    return tokens, queries


class QuarterSum:
    def __init__(self, low, high):
        size = lax.axis_size("dp")
        outer = size // QUARTERS
        self.hops = [(outer, 2 * outer), (2 * outer, outer)]
        step = 1
        while step < outer:
            self.hops.append((step, step))
            step *= 2
        self.size, self.pair, self.hop = size, (low, high), 0
        self.send()

    def send(self):
        self.came = [
            lax.ppermute(x, "dp", [(i, i ^ step) for i in range(self.size)])
            for x, step in zip(self.pair, self.hops[self.hop])
        ]

    def add(self, order):
        self.pair = order.add(*zip(self.pair, self.came))
        self.hop += 1
        if self.hop < len(self.hops):
            self.send()


def activation_rows(rows, tokens):
    blocks = lax.all_gather(rows, "mp", axis=0)
    holders, _, width = blocks.shape
    if holders != PIECES:
        blocks = jnp.concatenate(
            [
                blocks[:, :tokens].reshape(PIECES, -1, width),
                blocks[:, tokens:].reshape(PIECES, -1, width),
            ],
            axis=1,
        )
    return blocks.reshape(-1, width)


def shards(out_grads, inputs, out_basis, in_basis, query_out, query_in, damping):
    order = Order()
    dp, mp = lax.axis_index("dp"), lax.axis_index("mp")
    place = jnp.stack(
        [dp // (lax.axis_size("dp") // QUARTERS), mp % HALVES, mp // HALVES]
    ).astype(jnp.int32)

    tokens, queries = outer_rows(out_grads, query_out)
    length = tokens.shape[0] // HALVES
    low, high, act_rows = join_rows(order, tokens, queries, inputs, query_in)
    beside = [swap_quarter(low, 2), swap_quarter(high, 1)]
    behind = [swap_quarter(low, 1), swap_quarter(high, 2)]
    across = [swap_quarter(beside[0], 1), swap_quarter(beside[1], 2)]
    act_rows = activation_rows(act_rows, inputs.shape[0])

    width = out_basis.shape[1]
    lines = [LineSum(place, QUARTERS) for _ in range(streams_of(width))]
    held, acts = None, None
    chunks, late = [], []
    totals, swapped = [[] for _ in lines], [[] for _ in lines]

    def rotate(pair, unread=()):
        nonlocal held
        results = multiply(order, place, *pair, out_basis, held, unread)
        held = results.pop() if held is None else held
        came = [swap_core(x) for x in results[len(lines):]]
        chunks.append(list(zip(results, came)))

    def advance(s, unread=()):
        if s >= len(lines):
            return
        line, pins = lines[s], [*unread, *late]
        late.clear()
        chunk = chunks[line.step][s] if line.step < QUARTERS else None
        total = line.advance(order, chunk, pins)
        if total is not None:
            totals[s].append(total)
            swapped[s].append(swap_core(total))
            late.append(swapped[s][-1])

    def activate(unread=()):
        nonlocal acts
        acts = QuarterSum(*multiply_activations(order, act_rows, in_basis, unread))

    rotate((low, high))
    advance(0)
    advance(1)
    rotate(beside)
    advance(0)
    rotate(behind, [*behind])
    advance(1)
    rotate(across, [*across])
    advance(0)
    advance(1)
    activate()
    advance(0)
    advance(1, [act_rows])
    advance(0)
    acts.add(order)
    advance(1)
    advance(0)
    advance(1)
    advance(0)
    acts.add(order)
    advance(1)
    while acts.hop < len(acts.hops):
        acts.add(order)
    while len(totals[-1]) < QUARTERS:
        for s in range(len(lines)):
            advance(s)

    made = ()
    for s in range(len(lines)):
        rot = totals[s] + swapped[s]
        made = correct(order, length, place, damping, rot, acts.pair, s, width, made)
    return tuple(made)


def solution(mesh):
    placed = (
        P("dp", "mp"),
        P("mp", "dp"),
        P("mp", "dp"),
        P("dp", "mp"),
        P("dp", "mp"),
        P("mp", "dp"),
        P(),
    )
    return jax.shard_map(
        shards,
        mesh=mesh,
        in_specs=placed,
        out_specs=(P("dp", "mp"), P(None, "dp", "mp")),
        check_vma=False,
    )
```
